32 devices in a mesh: survey: 2 (over y), cell: 4 (over z), stn: 4 (over x, core).
Axes of the slice: x: 2, y: 2, z: 4, core: 2. Of those that a mesh axis runs over, the one named last changes fastest.
Arguments:
- densities: float32 [32768], P(('survey', 'cell', 'stn')), parts along dimension 0, may hold values from -6 to 6
- residual: float32 [6, 16384], P(None, ('survey', 'cell', 'stn')), parts along dimension 1, may hold values from -36 to 36
- direction: float32 [32768], P(('survey', 'cell', 'stn')), parts along dimension 0, may hold values from -36 to 36
- gradient_norm: float32 [2], P('survey'), parts along dimension 0, may hold values from 16384 to 131072
- station_place: float32 [3, 16384], P(None, ('survey', 'cell', 'stn')), parts along dimension 1, may hold values from -2 to 2, as said below
- cell_place: float32 [3, 32768], P(None, ('survey', 'cell', 'stn')), parts along dimension 1, may hold values from -2 to 2, as said below
- station_blocks: int32 [8, 4, 256], P(('survey', 'cell'), 'stn'), parts along dimension 0, may hold values from 0 to 15
- cell_blocks: int32 [8, 4, 256], P(('survey', 'cell'), 'stn'), parts along dimension 0, may hold values from 0 to 7
- pair_count: int32 [8, 4], P(('survey', 'cell'), 'stn'), parts along dimension 0, may hold values from 128 to 256, as said below
Outputs:
- densities_next: float32 [32768], P(('survey', 'cell', 'stn')), parts along dimension 0
- residual_next: float32 [6, 16384], P(None, ('survey', 'cell', 'stn')), parts along dimension 1
- direction_next: float32 [32768], P(('survey', 'cell', 'stn')), parts along dimension 0
- gradient_norm_next: float32 [2], P('survey'), parts along dimension 0
The draws below stay inside these ranges and needn't reach their ends.
There are 2 independent parts, one for each index of `survey`. The reference program is written for one: setup_inputs(seed, part) draws one part's arguments, and reference() takes and returns one part's arrays. A program takes and returns all parts, laid end to end along the dimension named above; each array names one. Nothing has to cross between parts.
Inputs may be any that keep to these rules, and one draw needn't show every extreme that they name: station_blocks[c, s, k] numbers a block of station group s as c' * 4 + b for block b of device (c', s). cell_blocks[c, s, k] numbers a block of cell group c as s' * 2 + b for block b of device (c, s'). Slots at or past pair_count hold valid block numbers and are ignored; in every survey some device holds 256 live slots. `station_place`: heights (third row) lie in 0.5 to 1.5. `cell_place`: depths (third row) lie in -1.5 to -0.5.
All inputs are finite; a program needn't handle non-finite values.
Results may differ from the reference program's by a relative error of at most 0.0003.
Values sent between devices are 32-bit elements; how exact they have to be, the bound alone decides.
No kernel may reach another device: no remote copies, remote signals or barrier semaphores. Data moves between devices by JAX's collectives and lax.ppermute only.
A program may use at most 64 MiB of HBM per device.

```python
import math
import jax
import jax.numpy as jnp
from jax import lax

SB_DEV = 4
CB_DEV = 2
PAIRS_DEV = 256
NSTAT = 8192
NCELL = 16384
N_CELL = 4
N_STN = 4


def rising_field(key, row_count, extent):
    first, second = jax.random.split(key)
    values = jnp.clip(jax.random.normal(first, (row_count, extent), jnp.float32), -4.0, 4.0)
    spread = jnp.exp(jax.random.uniform(second, (1, extent), jnp.float32) * math.log(3.0))
    ramp = jnp.exp(math.log(3.0) * jnp.arange(extent, dtype=jnp.float32) / extent)[None, :]
    return values * spread * ramp


def draw_residual(key, part):
    key = jax.random.fold_in(key, 11)
    return rising_field(key, 6, NSTAT)


def draw_direction(key, part):
    key = jax.random.fold_in(key, 12)
    return rising_field(key, 1, NCELL).reshape(NCELL)


def draw_station_place(key, part):
    key = jax.random.fold_in(key, 13)
    unit = jax.random.uniform(key, (3, NSTAT), jnp.float32, -1.0, 1.0)
    span = jnp.array([2.0, 2.0, 0.5], jnp.float32)[:, None]
    centre = jnp.array([0.0, 0.0, 1.0], jnp.float32)[:, None]
    return unit * span + centre


def draw_cell_place(key, part):
    key = jax.random.fold_in(key, 14)
    unit = jax.random.uniform(key, (3, NCELL), jnp.float32, -1.0, 1.0)
    span = jnp.array([2.0, 2.0, 0.5], jnp.float32)[:, None]
    centre = jnp.array([0.0, 0.0, -1.0], jnp.float32)[:, None]
    return unit * span + centre


def draw_pair_count(key, part):
    key = jax.random.fold_in(key, 15)
    first, second = jax.random.split(key)
    base = jax.random.randint(first, (N_CELL, N_STN), PAIRS_DEV // 2, PAIRS_DEV + 1)
    order = jax.random.permutation(second, N_CELL * N_STN).reshape(N_CELL, N_STN)
    heavy = order < max(1, N_CELL * N_STN // 8)
    return jnp.where(heavy, PAIRS_DEV, base).astype(jnp.int32)


def with_ends(drawn, stream_key, smallest, high):
    index_at = [jax.random.randint(jax.random.fold_in(stream_key, axis), (), 0, length) for axis, length in enumerate(drawn.shape)]
    longest = drawn.shape.index(max(drawn.shape))
    beside = index_at[:longest] + [(index_at[longest] + 1) % drawn.shape[longest]] + index_at[longest + 1:]
    return drawn.at[tuple(index_at)].set(smallest).at[tuple(beside)].set(high)


def level_of(own_key, shape, pieces, least, top_value):
    level = 1.0
    for axis_at, parts in pieces:
        draws = jax.random.uniform(jax.random.fold_in(jax.random.fold_in(own_key, 6), axis_at), (parts,), jnp.float32, least / len(pieces), top_value / len(pieces))
        level = level * jnp.repeat(jnp.exp(draws), shape[axis_at] // parts).reshape((-1,) + (1,) * (len(shape) - 1 - axis_at))
    return level


def normal_values(key, shape, scale, reach, cuts=(), held_as=jnp.bfloat16):
    level = level_of(key, shape, cuts, -0.22, 0.18) if cuts else 1.0
    values = jax.random.normal(key, shape, jnp.float32) * scale * level
    return jnp.minimum(jnp.maximum(values, -reach), reach).astype(held_as)


def setup_inputs(seed: int = 0, part: int = 0) -> dict:
    seeds = jax.random.split(jax.random.key(seed), 10)
    part_keys = jax.random.split(jax.random.fold_in(seeds[9], part), 10)
    densities = normal_values(part_keys[0], (NCELL,), 1.0, 6.0, ((0, 16),), jnp.float32)
    residual = draw_residual(jax.random.fold_in(jax.random.fold_in(seeds[9], part), 71), part)
    direction = draw_direction(jax.random.fold_in(jax.random.fold_in(seeds[9], part), 71), part)
    gradient_norm = jnp.clip(jnp.exp(jax.random.uniform(part_keys[3], (1,), jnp.float32, math.log(16384.0), math.log(131072.0))), 16384.0, 131072.0)
    station_place = draw_station_place(jax.random.fold_in(jax.random.fold_in(seeds[9], part), 71), part)
    cell_place = draw_cell_place(jax.random.fold_in(jax.random.fold_in(seeds[9], part), 71), part)
    station_blocks = with_ends(jax.random.randint(part_keys[6], (N_CELL, N_STN, PAIRS_DEV), 0, SB_DEV * N_CELL), jax.random.fold_in(part_keys[6], 1), 0, (SB_DEV * N_CELL) - 1).astype(jnp.int32)
    cell_blocks = with_ends(jax.random.randint(part_keys[7], (N_CELL, N_STN, PAIRS_DEV), 0, CB_DEV * N_STN), jax.random.fold_in(part_keys[7], 1), 0, (CB_DEV * N_STN) - 1).astype(jnp.int32)
    pair_count = draw_pair_count(jax.random.fold_in(jax.random.fold_in(seeds[9], part), 71), part)
    return {"densities": densities, "residual": residual, "direction": direction, "gradient_norm": gradient_norm, "station_place": station_place, "cell_place": cell_place, "station_blocks": station_blocks, "cell_blocks": cell_blocks, "pair_count": pair_count}


strength = 0.1

def tile_kernel(stations, prisms):
    offset_x = stations[0][:, None] - prisms[0][None, :]
    offset_y = stations[1][:, None] - prisms[1][None, :]
    offset_z = stations[2][:, None] - prisms[2][None, :]
    squared = offset_x * offset_x + offset_y * offset_y + offset_z * offset_z
    falloff = strength / (squared * squared * jnp.sqrt(squared))
    return jnp.stack([(3.0 * offset_x * offset_x - squared) * falloff, 3.0 * offset_x * offset_y * falloff, 3.0 * offset_x * offset_z * falloff, (3.0 * offset_y * offset_y - squared) * falloff, 3.0 * offset_y * offset_z * falloff, (3.0 * offset_z * offset_z - squared) * falloff])

def reference(densities, residual, direction, gradient_norm, station_place, cell_place, station_blocks, cell_blocks, pair_count):
    station_view = station_place.reshape(3, N_CELL, N_STN, SB_DEV, 128)
    prism_view = cell_place.reshape(3, N_CELL, N_STN * CB_DEV, 512)
    direction_view = direction.reshape(N_CELL, N_STN * CB_DEV, 512)
    all_slots = N_CELL * N_STN * PAIRS_DEV

    def locate(flat_index):
        flat_index = flat_index.astype(jnp.int32)
        device = flat_index // PAIRS_DEV
        position = flat_index % PAIRS_DEV
        cell_rank = device // N_STN
        station_rank = device % N_STN
        one_station = station_blocks[cell_rank, station_rank, position]
        one_cell = cell_blocks[cell_rank, station_rank, position]
        owner_rank = one_station // SB_DEV
        within = one_station % SB_DEV
        live = position < pair_count[cell_rank, station_rank]
        kernels = tile_kernel(station_view[:, owner_rank, station_rank, within, :], prism_view[:, cell_rank, one_cell, :])
        return (cell_rank, station_rank, one_cell, owner_rank, within, live, kernels)

    def forward_turn(flat_index, totals):
        cell_rank, station_rank, one_cell, owner_rank, within, live, kernels = locate(flat_index)
        values = direction_view[cell_rank, one_cell]
        contrib = jnp.where(live, lax.optimization_barrier(jnp.sum(kernels * values[None, None, :], axis=2)), 0.0)
        return totals.at[:, owner_rank, station_rank, within, :].add(contrib)
    image = lax.fori_loop(0, all_slots, forward_turn, jnp.zeros((6, N_CELL, N_STN, SB_DEV, 128), jnp.float32))
    image = image.reshape(6, -1)
    step_size = gradient_norm[0] / jnp.sum(image * image)
    densities_next = densities + step_size * direction
    residual_next = residual - step_size * image
    residual_view = residual_next.reshape(6, N_CELL, N_STN, SB_DEV, 128)

    def adjoint_turn(flat_index, totals):
        cell_rank, station_rank, one_cell, owner_rank, within, live, kernels = locate(flat_index)
        values = residual_view[:, owner_rank, station_rank, within, :]
        contrib = jnp.where(live, lax.optimization_barrier(jnp.sum(kernels * values[:, :, None], axis=(0, 1))), 0.0)
        return totals.at[cell_rank, one_cell].add(contrib)
    gradient = lax.fori_loop(0, all_slots, adjoint_turn, jnp.zeros((N_CELL, N_STN * CB_DEV, 512), jnp.float32))
    gradient = gradient.reshape(-1)
    norm_next = jnp.sum(gradient * gradient)
    direction_next = gradient + norm_next / gradient_norm[0] * direction
    return (densities_next, residual_next, direction_next, norm_next.reshape(1))
```

```python
import jax
import jax.numpy as jnp
from jax import lax
from jax.experimental import pallas as pl
from jax.experimental.pallas import tpu as pltpu
from jax.sharding import PartitionSpec as P

STATIONS = 128
CELLS = 512
SPAN = 2048
DEPTH = 32
STRENGTH = 0.1
F32 = jnp.float32
BF16 = jnp.bfloat16
NN = (((1,), (0,)), ((), ()))
NT = (((1,), (1,)), ((), ()))
VMEM_BYTES = 56 * 2**20


def rounded(value):
    return value.astype(BF16).astype(F32)


def three_parts(value):
    high = rounded(value)
    middle = rounded(value - high)
    return high, middle, value - high - middle


def multiply(left, right, numbers=NN):
    return lax.dot_general(left, right, numbers, preferred_element_type=F32)


def falloff_parts(squared):
    root = lax.rsqrt(squared)
    second = root * root
    falloff = second * second * root
    high = falloff.astype(BF16)
    return high, (falloff - high.astype(F32)).astype(BF16)


def square_sum(place):
    return place[0:1] * place[0:1] + place[1:2] * place[1:2] + place[2:3] * place[2:3]


def fill_station_rows(rows, place):
    high, middle, low = three_parts(place)
    norms = three_parts(square_sum(place))
    ones = jnp.ones_like(norms[0])
    for at, part in enumerate((high, high, middle, middle, high, low)):
        rows[3 * at : 3 * at + 3, :] = part
    for at, part in enumerate((*norms, ones, ones, ones)):
        rows[18 + at : 19 + at, :] = part
    rows[24:DEPTH, :] = jnp.zeros((DEPTH - 24, place.shape[1]), F32)


def fill_cell_rows(rows, place):
    high, middle, low = three_parts(-2.0 * place)
    norms = three_parts(square_sum(place))
    ones = jnp.ones_like(norms[0])
    for at, part in enumerate((high, middle, high, middle, low, high)):
        rows[3 * at : 3 * at + 3, :] = part
    for at, part in enumerate((ones, ones, ones, *norms)):
        rows[18 + at : 19 + at, :] = part
    rows[24:DEPTH, :] = jnp.zeros((DEPTH - 24, place.shape[1]), F32)


def join(target, pieces, rows):
    at = 0
    for piece in pieces:
        width = piece.shape[1]
        target[0:rows, at : at + width] = piece[0:rows, :]
        at += width


def transpose_into(target, rows):
    for at in range(0, rows.shape[1], 512):
        target[at : at + 512, :] = rows[:, at : at + 512].T.astype(BF16)


def listed_counts(info, station_list, cell_list, station_groups, blocks):
    slots = station_list.shape[1]
    station_total, cell_total = blocks
    per_cell = station_total // station_groups
    station_id = (
        lax.bitwise_xor(station_list[...] // per_cell, info[0]) * per_cell
        + station_list[...] % per_cell
    )
    cell_id = lax.bitwise_xor(cell_list[...] // 2, info[1]) * 2 + cell_list[...] % 2
    live = lax.broadcasted_iota(jnp.int32, (1, slots), 1) < info[2]
    cell_hot = (lax.broadcasted_iota(jnp.int32, (cell_total, slots), 0) == cell_id) & live
    station_hot = lax.broadcasted_iota(jnp.int32, (station_total, slots), 0) == station_id
    count = multiply(cell_hot.astype(F32).astype(BF16), station_hot.astype(F32).astype(BF16), NT)
    wide = (station_total, station_total * STATIONS)
    spread = lax.broadcasted_iota(jnp.int32, wide, 0) == (
        lax.broadcasted_iota(jnp.int32, wide, 1) // STATIONS
    )
    return multiply(count.astype(BF16), spread.astype(F32).astype(BF16))


def forward_kernel(station_pieces, cell_pieces, info, station_list, cell_list, *refs):
    station_refs = refs[:station_pieces]
    cell_refs = refs[station_pieces : station_pieces + cell_pieces]
    image, count, station, cell, station_rows, cell_rows, left, right, source, moments = refs[
        station_pieces + cell_pieces :
    ]
    width, extent = station.shape[1], cell.shape[1]
    join(station, station_refs, 3)
    join(cell, cell_refs, 4)
    count[...] = listed_counts(
        info,
        station_list,
        cell_list,
        width // CELLS,
        (width // STATIONS, extent // CELLS),
    )
    fill_station_rows(station_rows, station[0:3, :])
    right[...] = station_rows[...].astype(BF16)
    fill_cell_rows(cell_rows, cell[0:3, :])
    transpose_into(left, cell_rows)
    value = cell[3:4, :]
    x, y, z = cell[0:1, :], cell[1:2, :], cell[2:3, :]
    vx, vy, vz = value * x, value * y, value * z
    products = (value, vx, vy, vz, vx * x, vx * y, vx * z, vy * y, vy * z, vz * z)
    for at, row in enumerate(products):
        cell_rows[at : at + 1, :] = row
    cell_rows[10:16, :] = jnp.zeros((6, extent), F32)
    parts = three_parts(cell_rows[0:16, :])
    source[...] = jnp.concatenate([part.astype(BF16) for part in parts], axis=0)
    moments[...] = jnp.zeros_like(moments)
    spans = width // SPAN

    def turn(which, carry):
        block = which // spans
        lanes = pl.ds(pl.multiple_of(which % spans * SPAN, SPAN), SPAN)
        cells = pl.ds(pl.multiple_of(block * CELLS, CELLS), CELLS)
        squared = multiply(left[cells, :], right[:, lanes])
        high, low = falloff_parts(squared)
        weights = source[:, cells]
        total = multiply(weights, high) + multiply(weights, low)
        total = total[0:16] + total[16:32] + total[32:48]
        moments[:, lanes] += total * count[pl.ds(block, 1), lanes]
        return carry

    lax.fori_loop(0, spans * (extent // CELLS), turn, 0)
    sx, sy, sz = station[0:1, :], station[1:2, :], station[2:3, :]
    total, mx, my, mz, mxx, mxy, mxz, myy, myz, mzz = (moments[k : k + 1, :] for k in range(10))
    xx = sx * (sx * total - 2.0 * mx) + mxx
    yy = sy * (sy * total - 2.0 * my) + myy
    zz = sz * (sz * total - 2.0 * mz) + mzz
    xy = sx * (sy * total - my) - sy * mx + mxy
    xz = sx * (sz * total - mz) - sz * mx + mxz
    yz = sy * (sz * total - mz) - sz * my + myz
    image[0:1, :] = STRENGTH * (2.0 * xx - yy - zz)
    image[1:2, :] = (3.0 * STRENGTH) * xy
    image[2:3, :] = (3.0 * STRENGTH) * xz
    image[3:4, :] = STRENGTH * (2.0 * yy - xx - zz)
    image[4:5, :] = (3.0 * STRENGTH) * yz
    image[5:6, :] = STRENGTH * (2.0 * zz - xx - yy)
    image[6:8, :] = jnp.zeros((2, width), F32)


def tree(values):
    values = list(values)
    while len(values) > 1:
        values = [values[k] + values[k + 1] for k in range(0, len(values), 2)]
    return values[0]


def adjoint_kernel(station_pieces, cell_pieces, image_pieces, count, *refs):
    station_refs = refs[:station_pieces]
    at = station_pieces + cell_pieces
    cell_refs = refs[station_pieces:at]
    image_refs = refs[at : at + image_pieces]
    partial, own_image, station, cell, image, station_rows, cell_rows, left, right, vectors = refs[
        at + image_pieces :
    ]
    width, extent = station.shape[1], cell.shape[1]
    join(station, station_refs, 9)
    join(cell, cell_refs, 3)
    if image_pieces == 1:
        image[...] = image_refs[0][...]
        norm = jnp.sum(image[...] * image[...])
    else:
        part = width // image_pieces
        norms = []
        for k in range(image_pieces):
            block = tree(
                image_refs[other][:, (k ^ other) * part : ((k ^ other) + 1) * part]
                for other in range(image_pieces)
            )
            image[:, k * part : (k + 1) * part] = block
            norms.append(jnp.sum(block * block))
        norm = tree(norms)
    own_image[...] = image[:, 0 : own_image.shape[1]]
    fill_cell_rows(cell_rows, cell[0:3, :])
    right[...] = cell_rows[...].astype(BF16)
    fill_station_rows(station_rows, station[0:3, :])
    transpose_into(left, station_rows)
    sx, sy, sz = station[0:1, :], station[1:2, :], station[2:3, :]
    for first, source, offset in ((0, station, 3), (10, image, 0)):
        r = [STRENGTH * source[offset + k : offset + k + 1, :] for k in range(6)]
        axx, ayy, azz = 2.0 * r[0] - r[3] - r[5], 2.0 * r[3] - r[0] - r[5], 2.0 * r[5] - r[0] - r[3]
        axy, axz, ayz = 3.0 * r[1], 3.0 * r[2], 3.0 * r[4]
        whole = (
            sx * (axx * sx + axy * sy + axz * sz) + sy * (ayy * sy + ayz * sz) + azz * sz * sz
        )
        bx = 2.0 * axx * sx + axy * sy + axz * sz
        by = 2.0 * ayy * sy + axy * sx + ayz * sz
        bz = 2.0 * azz * sz + axz * sx + ayz * sy
        for k, row in enumerate((whole, bx, by, bz, axx, axy, axz, ayy, ayz, azz)):
            vectors[first + k : first + k + 1, :] = row
    vectors[20:24, :] = jnp.zeros((4, width), F32)
    partial[...] = jnp.zeros_like(partial)
    partial[:, CELLS:] = jnp.full((partial.shape[0], partial.shape[1] - CELLS), norm, F32)
    blocks = extent // CELLS

    def turn(block, carry):
        cells = pl.ds(pl.multiple_of(block * CELLS, CELLS), CELLS)

        def span_turn(which, sums):
            lanes = pl.ds(pl.multiple_of(which * SPAN, SPAN), SPAN)
            squared = multiply(left[lanes, :], right[:, cells])
            high, low = falloff_parts(squared)
            parts = three_parts(vectors[:, lanes] * count[pl.ds(block, 1), lanes])
            weights = jnp.concatenate(parts, axis=0).astype(BF16)
            total = multiply(weights, high) + multiply(weights, low)
            return sums + (total[0:24] + total[24:48] + total[48:72])

        sums = jnp.zeros((24, CELLS), F32)
        if width == SPAN:
            sums = span_turn(0, sums)
        else:
            sums = lax.fori_loop(0, width // SPAN, span_turn, sums)
        x, y, z = cell[0:1, cells], cell[1:2, cells], cell[2:3, cells]
        for vector in range(2):
            whole, bx, by, bz, axx, axy, axz, ayy, ayz, azz = (
                sums[10 * vector + k : 10 * vector + k + 1] for k in range(10)
            )
            value = (
                whole
                + x * (x * axx + y * axy + z * axz - bx)
                + y * (y * ayy + z * ayz - by)
                + z * (z * azz - bz)
            )
            partial[pl.ds(vector * blocks + block, 1), 0:CELLS] = value
        return carry

    lax.fori_loop(0, blocks, turn, 0)


def update_kernel(pieces, gradient_norm, densities, direction, residual, image, *refs):
    partial_refs = refs[:pieces]
    densities_next, residual_next, gradient, norm = refs[pieces:]
    blocks = partial_refs[0].shape[0] // 2
    each = blocks // pieces
    step = gradient_norm[0] / tree(ref[0:1, CELLS : CELLS + 1] for ref in partial_refs)
    sums = []
    for k in range(pieces):
        both = [
            tree(
                partial_refs[other][
                    vector * blocks + (k ^ other) * each : vector * blocks + ((k ^ other) + 1) * each,
                    0:CELLS,
                ]
                for other in range(pieces)
            )
            for vector in range(2)
        ]
        block = both[0] - step * both[1]
        sums.append(jnp.sum(block * block, axis=(0, 1), keepdims=True))
        if k == 0:
            across = CELLS // 128
            for b in range(each):
                for u in range(across):
                    at = b * across + u
                    gradient[at : at + 1, :] = block[b : b + 1, u * 128 : (u + 1) * 128]
    norm[...] = jnp.broadcast_to(tree(sums), norm.shape)
    densities_next[...] = densities[...] + step * direction[...]
    residual_next[...] = residual[...] - step * image[0:6, :]


def exchanged(value, axis, size):
    return [value] + [
        lax.ppermute(value, axis, [(rank, rank ^ other) for rank in range(size)])
        for other in range(1, size)
    ]


def on_device(
    densities,
    residual,
    direction,
    gradient_norm,
    station_place,
    cell_place,
    station_blocks,
    cell_blocks,
    pair_count,
):
    cell_size, stn_size = lax.axis_size("cell"), lax.axis_size("stn")
    direct = cell_size <= 4
    station_own = jnp.concatenate([station_place, residual], axis=0)
    cell_own = jnp.concatenate([cell_place, direction[None]], axis=0)
    cell_parts = exchanged(cell_own, "stn", stn_size)
    if direct:
        station_parts = exchanged(station_own, "cell", cell_size)
        cell_rank = lax.axis_index("cell")
    else:
        station_parts = [lax.all_gather(station_own, "cell", axis=1, tiled=True)]
        cell_rank = jnp.int32(0)
    info = jnp.stack([cell_rank, lax.axis_index("stn"), pair_count.reshape(())])
    width = cell_size * station_own.shape[1]
    extent = stn_size * cell_own.shape[1]
    blocks = extent // CELLS
    in_vmem, in_smem = pl.BlockSpec(memory_space=pltpu.VMEM), pl.BlockSpec(memory_space=pltpu.SMEM)
    params = pltpu.CompilerParams(vmem_limit_bytes=VMEM_BYTES)
    pieces = len(station_parts) + len(cell_parts)

    def forward(*refs):
        forward_kernel(len(station_parts), len(cell_parts), *refs)

    image_part, count = pl.pallas_call(
        forward,
        out_shape=(
            jax.ShapeDtypeStruct((8, width), F32),
            jax.ShapeDtypeStruct((blocks, width), F32),
        ),
        in_specs=[in_smem] + [in_vmem] * (2 + pieces),
        out_specs=(in_vmem, in_vmem),
        scratch_shapes=[
            pltpu.VMEM((8, width), F32),
            pltpu.VMEM((8, extent), F32),
            pltpu.VMEM((DEPTH, width), F32),
            pltpu.VMEM((DEPTH, extent), F32),
            pltpu.VMEM((extent, DEPTH), BF16),
            pltpu.VMEM((DEPTH, width), BF16),
            pltpu.VMEM((48, extent), BF16),
            pltpu.VMEM((16, width), F32),
        ],
        compiler_params=params,
        name="forward",
    )(
        info,
        station_blocks.reshape(1, -1),
        cell_blocks.reshape(1, -1),
        *station_parts,
        *cell_parts,
    )
    if direct:
        image_parts = exchanged(image_part, "cell", cell_size)
    else:
        image_parts = [lax.psum(image_part, "cell")]

    def adjoint(*refs):
        adjoint_kernel(len(station_parts), len(cell_parts), len(image_parts), *refs)

    own = station_own.shape[1]
    partial, image_own = pl.pallas_call(
        adjoint,
        out_shape=(
            jax.ShapeDtypeStruct((2 * blocks, CELLS + 128), F32),
            jax.ShapeDtypeStruct((8, own if direct else width), F32),
        ),
        in_specs=[in_vmem] * (1 + pieces + len(image_parts)),
        out_specs=(in_vmem, in_vmem),
        scratch_shapes=[
            pltpu.VMEM((16, width), F32),
            pltpu.VMEM((8, extent), F32),
            pltpu.VMEM((8, width), F32),
            pltpu.VMEM((DEPTH, width), F32),
            pltpu.VMEM((DEPTH, extent), F32),
            pltpu.VMEM((width, DEPTH), BF16),
            pltpu.VMEM((DEPTH, extent), BF16),
            pltpu.VMEM((24, width), F32),
        ],
        compiler_params=params,
        name="adjoint",
    )(count, *station_parts, *cell_parts, *image_parts)
    if not direct:
        image_own = lax.dynamic_slice_in_dim(image_own, lax.axis_index("cell") * own, own, axis=1)
    partial_parts = exchanged(partial, "stn", stn_size)
    shape = (-1, 128)

    def update(*refs):
        update_kernel(stn_size, *refs)

    flat = direction.reshape(shape)
    densities_next, residual_next, gradient, norm_part = pl.pallas_call(
        update,
        out_shape=(
            jax.ShapeDtypeStruct(flat.shape, F32),
            jax.ShapeDtypeStruct(residual.shape, F32),
            jax.ShapeDtypeStruct(flat.shape, F32),
            jax.ShapeDtypeStruct((1, 128), F32),
        ),
        in_specs=[in_smem] + [in_vmem] * (4 + stn_size),
        out_specs=(in_vmem,) * 4,
        name="update",
    )(gradient_norm, densities.reshape(shape), flat, residual, image_own, *partial_parts)
    if direct:
        norm_next = tree(exchanged(norm_part, "cell", cell_size))
    else:
        norm_next = lax.psum(norm_part, "cell")
    direction_next = gradient + norm_next / gradient_norm[0] * flat
    return (
        densities_next.reshape(-1),
        residual_next,
        direction_next.reshape(-1),
        norm_next[0, 0:1],
    )


def solution(mesh):
    in_specs = (
        P(("survey", "cell", "stn")),
        P(None, ("survey", "cell", "stn")),
        P(("survey", "cell", "stn")),
        P("survey"),
        P(None, ("survey", "cell", "stn")),
        P(None, ("survey", "cell", "stn")),
        P(("survey", "cell"), "stn", None),
        P(("survey", "cell"), "stn", None),
        P(("survey", "cell"), "stn"),
    )
    out_specs = (
        P(("survey", "cell", "stn")),
        P(None, ("survey", "cell", "stn")),
        P(("survey", "cell", "stn")),
        P("survey"),
    )
    return jax.shard_map(
        on_device, mesh=mesh, in_specs=in_specs, out_specs=out_specs, check_vma=False
    )
```

```python
import jax
import jax.numpy as jnp
from jax import lax
from jax.experimental import pallas as pl
from jax.experimental.pallas import tpu as pltpu
from jax.sharding import PartitionSpec as P

STATIONS = 128
CELLS = 512
SPAN = 2048
DEPTH = 32
STRENGTH = 0.1
SHRINK = 2.0**-6
GROWN = 2.0**-15 * STRENGTH
TURN = 1024
F8_TOP = 256.0
F32 = jnp.float32
BF16 = jnp.bfloat16
F8 = jnp.float8_e4m3fn
NN = (((1,), (0,)), ((), ()))
NT = (((1,), (1,)), ((), ()))


def rounded(value):
    return value.astype(BF16).astype(F32)


def three_parts(value):
    high = rounded(value)
    middle = rounded(value - high)
    return high, middle, value - high - middle


def multiply(left, right, numbers=NN):
    return lax.dot_general(left, right, numbers, preferred_element_type=F32)


def falloff_parts(squared, low_type):
    root = lax.rsqrt(squared)
    second = root * root
    falloff = second * second * root
    high = falloff.astype(BF16)
    return high, (falloff - high.astype(F32)).astype(low_type)


def narrow_parts(value):
    top = jnp.maximum(jnp.max(jnp.abs(value), axis=1, keepdims=True), 1e-30)
    scaled = value * (F8_TOP / top)
    high = scaled.astype(F8).astype(F32)
    return high, (scaled - high) * 16.0, top * (1.0 / F8_TOP)


def square_sum(place):
    return place[0:1] * place[0:1] + place[1:2] * place[1:2] + place[2:3] * place[2:3]


def fill_station_rows(rows, place):
    high, middle, low = three_parts(place)
    norms = three_parts(square_sum(place))
    ones = jnp.ones_like(norms[0])
    for at, part in enumerate((high, high, middle, middle, high, low)):
        rows[3 * at : 3 * at + 3, :] = part
    for at, part in enumerate((*norms, ones, ones, ones)):
        rows[18 + at : 19 + at, :] = part
    rows[24:DEPTH, :] = jnp.zeros((DEPTH - 24, place.shape[1]), F32)


def fill_cell_rows(rows, place):
    high, middle, low = three_parts((-2.0 * SHRINK) * place)
    norms = three_parts(SHRINK * square_sum(place))
    ones = jnp.full_like(norms[0], SHRINK)
    for at, part in enumerate((high, middle, high, middle, low, high)):
        rows[3 * at : 3 * at + 3, :] = part
    for at, part in enumerate((ones, ones, ones, *norms)):
        rows[18 + at : 19 + at, :] = part
    rows[24:DEPTH, :] = jnp.zeros((DEPTH - 24, place.shape[1]), F32)


def join(target, pieces, rows):
    at = 0
    for piece in pieces:
        width = piece.shape[1]
        target[0:rows, at : at + width] = piece[0:rows, :]
        at += width


def transpose_into(target, rows):
    for at in range(0, rows.shape[1], 512):
        target[at : at + 512, :] = rows[:, at : at + 512].T.astype(BF16)


def pack(target, base, row):
    for at in range(row.shape[1] // 128):
        target[base + at : base + at + 1, :] = row[:, at * 128 : (at + 1) * 128]


def unpack(target, row, lane, source):
    for at in range(source.shape[0]):
        start = lane + at * 128
        target[row : row + 1, start : start + 128] = source[at : at + 1, :]


def listed_tiles(station_list, cell_list, filled, ranks, own_blocks):
    per_cell, per_stn = own_blocks
    station_id = (
        lax.bitwise_xor(station_list // per_cell, ranks[0]) * per_cell + station_list % per_cell
    )
    cell_id = lax.bitwise_xor(cell_list // per_stn, ranks[1]) * per_stn + cell_list % per_stn
    live = lax.broadcasted_iota(jnp.int32, cell_list.shape, 1) < filled
    return jnp.concatenate([station_id, jnp.where(live, cell_id, -1)], axis=0)


def listed_counts(tiles, station_total, cell_total):
    slots = tiles.shape[1]
    station_hot = lax.broadcasted_iota(jnp.int32, (station_total, slots), 0) == tiles[0:1, :]
    cell_hot = lax.broadcasted_iota(jnp.int32, (cell_total, slots), 0) == tiles[1:2, :]
    count = multiply(cell_hot.astype(F32).astype(BF16), station_hot.astype(F32).astype(BF16), NT)
    wide = (station_total, station_total * STATIONS)
    spread = lax.broadcasted_iota(jnp.int32, wide, 0) == (
        lax.broadcasted_iota(jnp.int32, wide, 1) // STATIONS
    )
    return multiply(count.astype(BF16), spread.astype(F32).astype(BF16))


def forward_kernel(station_pieces, cell_pieces, keep, tiles, residual, *refs):
    station_refs = refs[:station_pieces]
    refs = refs[station_pieces:]
    cell_refs = refs[:cell_pieces]
    image, count, station, cell, *outs = refs[cell_pieces:]
    kept = outs[:2] if keep else None
    station_rows, cell_rows, left, right, source, narrow, moments = outs[2 if keep else 0 :]
    width, extent = station.shape[1], cell.shape[1]
    join(cell, cell_refs, 4)
    join(station, station_refs, 3 if keep else 9)
    count[...] = listed_counts(tiles, width // STATIONS, extent // CELLS)
    fill_station_rows(station_rows, station[0:3, :])
    right[...] = station_rows[...].astype(BF16)
    fill_cell_rows(cell_rows, cell[0:3, :])
    transpose_into(left, cell_rows)
    value = cell[3:4, :]
    x, y, z = cell[0:1, :], cell[1:2, :], cell[2:3, :]
    vx, vy, vz = value * x, value * y, value * z
    products = (value, vx, vy, vz, vx * x, vx * y, vx * z, vy * y, vy * z, vz * z)
    for at, row in enumerate(products):
        cell_rows[at : at + 1, :] = row
    cell_rows[10:16, :] = jnp.zeros((6, extent), F32)
    parts = three_parts(cell_rows[0:16, :])
    source[...] = jnp.concatenate([part.astype(BF16) for part in parts], axis=0)
    high, low, unit = narrow_parts(cell_rows[0:16, :])
    narrow[...] = jnp.concatenate([high, low], axis=0).astype(F8)
    moments[...] = jnp.zeros_like(moments)
    spans = width // SPAN

    def turn(which, carry):
        group = which // spans
        lanes = pl.ds(pl.multiple_of(which % spans * SPAN, SPAN), SPAN)
        cells = pl.ds(pl.multiple_of(group * TURN, TURN), TURN)
        squared = multiply(left[cells, :], right[:, lanes])
        high, low = falloff_parts(squared, F8)
        if keep:
            kept[0][cells, :] = high
            kept[1][cells, :] = low
        sums = moments[:, lanes]
        for at in range(TURN // CELLS):
            block = group * (TURN // CELLS) + at
            here = pl.ds(pl.multiple_of(block * CELLS, CELLS), CELLS)
            rows = slice(at * CELLS, (at + 1) * CELLS)
            wide = multiply(source[:, here], high[rows])
            fine = multiply(narrow[:, here], low[rows])
            total = wide[0:16] + wide[16:32] + wide[32:48]
            total = total + (fine[0:16] + fine[16:32] * (1.0 / 16.0)) * unit
            sums = sums + total * count[pl.ds(block, 1), lanes]
        moments[:, lanes] = sums
        return carry

    lax.fori_loop(0, spans * (extent // TURN), turn, 0)
    sx, sy, sz = station[0:1, :], station[1:2, :], station[2:3, :]
    total, mx, my, mz, mxx, mxy, mxz, myy, myz, mzz = (moments[k : k + 1, :] for k in range(10))
    xx = sx * (sx * total - 2.0 * mx) + mxx
    yy = sy * (sy * total - 2.0 * my) + myy
    zz = sz * (sz * total - 2.0 * mz) + mzz
    xy = sx * (sy * total - my) - sy * mx + mxy
    xz = sx * (sz * total - mz) - sz * mx + mxz
    yz = sy * (sz * total - mz) - sz * my + myz
    rows = (2.0 * xx - yy - zz, 3.0 * xy, 3.0 * xz, 2.0 * yy - xx - zz, 3.0 * yz)
    for k, row in enumerate(rows):
        pack(image, k * (width // 128), GROWN * row)
    if keep:
        image[5 * (width // 128) :, :] = residual[...]


def tree(values):
    values = list(values)
    while len(values) > 1:
        values = [values[k] + values[k + 1] for k in range(0, len(values), 2)]
    return values[0]


def gather_images(image, residual, image_refs, own):
    width = image.shape[1]
    rows, each = width // 128, own // 128
    norms = []
    for owner in range(width // own):
        blocks = []
        for k in range(5):
            blocks.append(
                tree(
                    ref[k * rows + (owner ^ other) * each : k * rows + ((owner ^ other) + 1) * each, :]
                    for other, ref in enumerate(image_refs)
                )
            )
        blocks.append(-(blocks[0] + blocks[3]))
        squares = 0.0
        for k, block in enumerate(blocks):
            unpack(image, k, owner * own, block)
            squares = squares + block * block
        norms.append(jnp.sum(squares))
    if residual is not None:
        for other, ref in enumerate(image_refs):
            for k in range(6):
                first = 5 * rows + k * each
                unpack(residual, k, other * own, ref[first : first + each, :])
    return tree(norms)


def fill_vectors(vectors, station, residual, image):
    sx, sy, sz = station[0:1, :], station[1:2, :], station[2:3, :]
    for first, source, offset in ((0, *residual), (10, *image)):
        r = [GROWN * source[offset + k : offset + k + 1, :] for k in range(6)]
        axx, ayy, azz = 2.0 * r[0] - r[3] - r[5], 2.0 * r[3] - r[0] - r[5], 2.0 * r[5] - r[0] - r[3]
        axy, axz, ayz = 3.0 * r[1], 3.0 * r[2], 3.0 * r[4]
        whole = (
            sx * (axx * sx + axy * sy + axz * sz) + sy * (ayy * sy + ayz * sz) + azz * sz * sz
        )
        bx = 2.0 * axx * sx + axy * sy + axz * sz
        by = 2.0 * ayy * sy + axy * sx + ayz * sz
        bz = 2.0 * azz * sz + axz * sx + ayz * sy
        for k, row in enumerate((whole, bx, by, bz, axx, axy, axz, ayy, ayz, azz)):
            vectors[first + k : first + k + 1, :] = row
    vectors[20:24, :] = jnp.zeros((4, vectors.shape[1]), F32)


def start_partial(partial, norm):
    side = partial.shape[1] - CELLS
    partial[:, CELLS:] = jnp.full((partial.shape[0], side), norm, F32)


def write_partial(partial, sums, place, block, blocks):
    x, y, z = place[0:1], place[1:2], place[2:3]
    for vector in range(2):
        whole, bx, by, bz, axx, axy, axz, ayy, ayz, azz = (
            sums[10 * vector + k : 10 * vector + k + 1] for k in range(10)
        )
        value = (
            whole
            + x * (x * axx + y * axy + z * axz - bx)
            + y * (y * ayy + z * ayz - by)
            + z * (z * azz - bz)
        )
        partial[pl.ds(vector * blocks + block, 1), 0:CELLS] = value


def kept_adjoint_kernel(count, station, cell, high, low, *refs):
    *image_refs, partial, own_image, image, residual, vectors = refs
    extent, own = cell.shape[1], own_image.shape[1]
    norm = gather_images(image, residual, image_refs, own)
    own_image[...] = image[:, 0:own]
    fill_vectors(vectors, station, (residual, 0), (image, 0))
    start_partial(partial, norm)
    blocks = extent // CELLS

    def turn(group, carry):
        for at in range(TURN // CELLS):
            block = group * (TURN // CELLS) + at
            cells = pl.ds(pl.multiple_of(block * CELLS, CELLS), CELLS)
            counted = vectors[...] * count[pl.ds(block, 1), :]
            weights = jnp.concatenate(three_parts(counted), axis=0).astype(BF16)
            above, below, unit = narrow_parts(counted)
            narrow = jnp.concatenate([above, below], axis=0).astype(F8)
            wide = multiply(high[cells, :], weights, NT).T
            fine = multiply(low[cells, :], narrow, NT).T
            sums = wide[0:24] + wide[24:48] + wide[48:72]
            sums = sums + (fine[0:24] + fine[24:48] * (1.0 / 16.0)) * unit
            write_partial(partial, sums, cell[0:3, cells], block, blocks)
        return carry

    lax.fori_loop(0, extent // TURN, turn, 0)


def adjoint_kernel(count, station, cell, image_ref, *refs):
    partial, own_image, image, station_rows, cell_rows, left, right, vectors = refs
    width, extent = station.shape[1], cell.shape[1]
    norm = gather_images(image, None, [image_ref], CELLS)
    own_image[...] = image[...]
    fill_cell_rows(cell_rows, cell[0:3, :])
    right[...] = cell_rows[...].astype(BF16)
    fill_station_rows(station_rows, station[0:3, :])
    transpose_into(left, station_rows)
    fill_vectors(vectors, station, (station, 3), (image, 0))
    start_partial(partial, norm)
    blocks = extent // CELLS

    def turn(block, carry):
        cells = pl.ds(pl.multiple_of(block * CELLS, CELLS), CELLS)

        def span_turn(which, sums):
            lanes = pl.ds(pl.multiple_of(which * SPAN, SPAN), SPAN)
            squared = multiply(left[lanes, :], right[:, cells])
            high, low = falloff_parts(squared, BF16)
            parts = three_parts(vectors[:, lanes] * count[pl.ds(block, 1), lanes])
            weights = jnp.concatenate(parts, axis=0).astype(BF16)
            total = multiply(weights, high) + multiply(weights, low)
            return sums + (total[0:24] + total[24:48] + total[48:72])

        sums = lax.fori_loop(0, width // SPAN, span_turn, jnp.zeros((24, CELLS), F32))
        write_partial(partial, sums, cell[0:3, cells], block, blocks)
        return carry

    lax.fori_loop(0, blocks, turn, 0)


def update_kernel(pieces, gradient_norm, densities, direction, residual, image, *refs):
    partial_refs = refs[:pieces]
    densities_next, residual_next, gradient, norm = refs[pieces:]
    blocks = partial_refs[0].shape[0] // 2
    each = blocks // pieces
    step = gradient_norm[0] / tree(ref[0:1, CELLS : CELLS + 1] for ref in partial_refs)
    sums = []
    for k in range(pieces):
        both = [
            tree(
                partial_refs[other][
                    vector * blocks + (k ^ other) * each : vector * blocks + ((k ^ other) + 1) * each,
                    0:CELLS,
                ]
                for other in range(pieces)
            )
            for vector in range(2)
        ]
        block = both[0] - step * both[1]
        sums.append(jnp.sum(block * block, axis=(0, 1), keepdims=True))
        if k == 0:
            for b in range(each):
                pack(gradient, b * (CELLS // 128), block[b : b + 1, :])
    norm[...] = jnp.broadcast_to(tree(sums), norm.shape)
    densities_next[...] = densities[...] + step * direction[...]
    residual_next[...] = residual[...] - step * image[0:6, :]


def finish_kernel(gradient_norm, gradient, direction, *refs):
    *norms, direction_next, norm_next = refs
    total = tree(ref[...] for ref in norms)
    direction_next[...] = gradient[...] + total / gradient_norm[0] * direction[...]
    norm_next[0] = total[0, 0]


def sent(value, axis, size, other):
    return lax.ppermute(value, axis, [(rank, rank ^ other) for rank in range(size)])


def doubled(value, axis, size):
    step = 1
    while step < size // 2:
        value = jnp.concatenate([value, sent(value, axis, size, step)], axis=1)
        step *= 2
    return [value, sent(value, axis, size, step)]


def exchanged(value, axis, size):
    return [value] + [sent(value, axis, size, other) for other in range(1, size)]


def on_device(
    densities,
    residual,
    direction,
    gradient_norm,
    station_place,
    cell_place,
    station_blocks,
    cell_blocks,
    pair_count,
):
    cell_size, stn_size = lax.axis_size("cell"), lax.axis_size("stn")
    direct = cell_size <= 4
    own, cell_own = station_place.shape[1], cell_place.shape[1]
    width, extent = cell_size * own, stn_size * cell_own
    rows, blocks = width // 128, extent // CELLS
    ranks = (lax.axis_index("cell") if direct else 0, lax.axis_index("stn"))
    tiles = listed_tiles(
        station_blocks.reshape(1, -1),
        cell_blocks.reshape(1, -1),
        pair_count.reshape(()),
        ranks,
        (own // STATIONS, cell_own // CELLS),
    )
    if direct:
        station_parts = doubled(station_place, "cell", cell_size)
    else:
        both = jnp.concatenate([station_place, residual], axis=0)
        station_parts = [lax.all_gather(both, "cell", axis=1, tiled=True)]
    cell_mine = jnp.concatenate([cell_place, direction[None]], axis=0)
    cell_parts = doubled(cell_mine, "stn", stn_size)
    in_vmem, in_smem = pl.BlockSpec(memory_space=pltpu.VMEM), pl.BlockSpec(memory_space=pltpu.SMEM)
    params = pltpu.CompilerParams(vmem_limit_bytes=(16 if direct else 56) * 2**20)
    small = pltpu.CompilerParams(vmem_limit_bytes=2**20)
    counts = (len(station_parts), len(cell_parts))
    pieces = sum(counts)

    def forward(*refs):
        forward_kernel(*counts, direct, *refs)

    out_shape = [
        jax.ShapeDtypeStruct((5 * rows + (6 * own // 128 if direct else 0), 128), F32),
        jax.ShapeDtypeStruct((blocks, width), F32),
        jax.ShapeDtypeStruct((16, width), F32),
        jax.ShapeDtypeStruct((8, extent), F32),
    ]
    if direct:
        out_shape += [
            jax.ShapeDtypeStruct((extent, width), BF16),
            jax.ShapeDtypeStruct((extent, width), F8),
        ]
    image_part, *kept = pl.pallas_call(
        forward,
        out_shape=out_shape,
        in_specs=[in_vmem] * (2 + pieces),
        out_specs=[in_vmem] * len(out_shape),
        scratch_shapes=[
            pltpu.VMEM((DEPTH, width), F32),
            pltpu.VMEM((DEPTH, extent), F32),
            pltpu.VMEM((extent, DEPTH), BF16),
            pltpu.VMEM((DEPTH, width), BF16),
            pltpu.VMEM((48, extent), BF16),
            pltpu.VMEM((32, extent), F8),
            pltpu.VMEM((16, width), F32),
        ],
        compiler_params=params,
        name="forward",
    )(tiles, residual.reshape(-1, 128), *station_parts, *cell_parts)
    if direct:
        image_parts = exchanged(image_part, "cell", cell_size)
    else:
        image_parts = [lax.psum(image_part, "cell")]

    def adjoint(*refs):
        (kept_adjoint_kernel if direct else adjoint_kernel)(*refs)

    if direct:
        scratch = [pltpu.VMEM((8, width), F32)]
    else:
        scratch = [
            pltpu.VMEM((DEPTH, width), F32),
            pltpu.VMEM((DEPTH, extent), F32),
            pltpu.VMEM((width, DEPTH), BF16),
            pltpu.VMEM((DEPTH, extent), BF16),
        ]
    partial, image_own = pl.pallas_call(
        adjoint,
        out_shape=(
            jax.ShapeDtypeStruct((2 * blocks, CELLS + 128), F32),
            jax.ShapeDtypeStruct((8, own if direct else width), F32),
        ),
        in_specs=[in_vmem] * (len(kept) + len(image_parts)),
        out_specs=(in_vmem, in_vmem),
        scratch_shapes=[
            pltpu.VMEM((8, width), F32),
            *scratch,
            pltpu.VMEM((24, width), F32),
        ],
        compiler_params=params,
        name="adjoint",
    )(*kept, *image_parts)
    if not direct:
        image_own = lax.dynamic_slice_in_dim(image_own, lax.axis_index("cell") * own, own, axis=1)
    partial_parts = exchanged(partial, "stn", stn_size)

    def update(*refs):
        update_kernel(stn_size, *refs)

    flat = direction.reshape(-1, 128)
    densities_next, residual_next, gradient, norm_part = pl.pallas_call(
        update,
        out_shape=(
            jax.ShapeDtypeStruct(flat.shape, F32),
            jax.ShapeDtypeStruct(residual.shape, F32),
            jax.ShapeDtypeStruct(flat.shape, F32),
            jax.ShapeDtypeStruct((1, 128), F32),
        ),
        in_specs=[in_smem] + [in_vmem] * (4 + stn_size),
        out_specs=(in_vmem,) * 4,
        compiler_params=small,
        name="update",
    )(gradient_norm, densities.reshape(flat.shape), flat, residual, image_own, *partial_parts)
    if direct:
        norm_parts = exchanged(norm_part, "cell", cell_size)
    else:
        norm_parts = [lax.psum(norm_part, "cell")]
    direction_next, norm_next = pl.pallas_call(
        finish_kernel,
        out_shape=(
            jax.ShapeDtypeStruct(flat.shape, F32),
            jax.ShapeDtypeStruct((1,), F32),
        ),
        in_specs=[in_smem] + [in_vmem] * (2 + len(norm_parts)),
        out_specs=(in_vmem, in_smem),
        compiler_params=small,
        name="finish",
    )(gradient_norm, gradient, flat, *norm_parts)
    return (densities_next.reshape(-1), residual_next, direction_next.reshape(-1), norm_next)


def solution(mesh):
    in_specs = (
        P(("survey", "cell", "stn")),
        P(None, ("survey", "cell", "stn")),
        P(("survey", "cell", "stn")),
        P("survey"),
        P(None, ("survey", "cell", "stn")),
        P(None, ("survey", "cell", "stn")),
        P(("survey", "cell"), "stn", None),
        P(("survey", "cell"), "stn", None),
        P(("survey", "cell"), "stn"),
    )
    out_specs = (
        P(("survey", "cell", "stn")),
        P(None, ("survey", "cell", "stn")),
        P(("survey", "cell", "stn")),
        P("survey"),
    )
    return jax.shard_map(
        on_device, mesh=mesh, in_specs=in_specs, out_specs=out_specs, check_vma=False
    )
```

```python
import jax
import jax.numpy as jnp
from jax import lax
from jax.experimental import pallas as pl
from jax.experimental.pallas import tpu as pltpu
from jax.sharding import PartitionSpec as P

STATIONS = 128
CELLS = 512
SPAN = 2048
DEPTH = 32
STRENGTH = 0.1
SHRINK = 2.0**-6
GROWN = 2.0**-15 * STRENGTH
TURN = 1024
BLOCKS_A_TURN = 8
F8_TOP = 256.0
F32 = jnp.float32
BF16 = jnp.bfloat16
F8 = jnp.float8_e4m3fn
NN = (((1,), (0,)), ((), ()))
NT = (((1,), (1,)), ((), ()))


def rounded(value):
    return value.astype(BF16).astype(F32)


def three_parts(value):
    high = rounded(value)
    middle = rounded(value - high)
    return high, middle, value - high - middle


def multiply(left, right, numbers=NN):
    return lax.dot_general(left, right, numbers, preferred_element_type=F32)


def falloff_parts(squared, low_type):
    root = lax.rsqrt(squared)
    second = root * root
    falloff = second * second * root
    high = falloff.astype(BF16)
    return high, (falloff - high.astype(F32)).astype(low_type)


def narrow_parts(value):
    top = jnp.maximum(jnp.max(jnp.abs(value), axis=1, keepdims=True), 1e-30)
    scaled = value * (F8_TOP / top)
    high = scaled.astype(F8).astype(F32)
    return high, (scaled - high) * 16.0, top * (1.0 / F8_TOP)


def square_sum(place):
    return place[0:1] * place[0:1] + place[1:2] * place[1:2] + place[2:3] * place[2:3]


def fill_station_rows(rows, place):
    high, middle, low = three_parts(place)
    norms = three_parts(square_sum(place))
    ones = jnp.ones_like(norms[0])
    for at, part in enumerate((high, high, middle, middle, high, low)):
        rows[3 * at : 3 * at + 3, :] = part
    for at, part in enumerate((*norms, ones, ones, ones)):
        rows[18 + at : 19 + at, :] = part
    rows[24:DEPTH, :] = jnp.zeros((DEPTH - 24, place.shape[1]), F32)


def fill_cell_rows(rows, place):
    high, middle, low = three_parts((-2.0 * SHRINK) * place)
    norms = three_parts(SHRINK * square_sum(place))
    ones = jnp.full_like(norms[0], SHRINK)
    for at, part in enumerate((high, middle, high, middle, low, high)):
        rows[3 * at : 3 * at + 3, :] = part
    for at, part in enumerate((ones, ones, ones, *norms)):
        rows[18 + at : 19 + at, :] = part
    rows[24:DEPTH, :] = jnp.zeros((DEPTH - 24, place.shape[1]), F32)


def join(target, pieces, rows):
    at = 0
    for piece in pieces:
        width = piece.shape[1]
        target[0:rows, at : at + width] = piece[0:rows, :]
        at += width


def transpose_into(target, rows):
    for at in range(0, rows.shape[1], 512):
        target[at : at + 512, :] = rows[:, at : at + 512].T.astype(BF16)


def pack(target, base, row):
    for at in range(row.shape[1] // 128):
        target[base + at : base + at + 1, :] = row[:, at * 128 : (at + 1) * 128]


def unpack(target, row, lane, source):
    for at in range(source.shape[0]):
        start = lane + at * 128
        target[row : row + 1, start : start + 128] = source[at : at + 1, :]


def listed_counts(station_list, cell_list, filled, ranks, blocks, own_blocks):
    slots = station_list.shape[1]
    station_total, cell_total = blocks
    per_cell, per_stn = own_blocks
    station_id = (
        lax.bitwise_xor(station_list[...] // per_cell, ranks[0]) * per_cell
        + station_list[...] % per_cell
    )
    cell_id = (
        lax.bitwise_xor(cell_list[...] // per_stn, ranks[1]) * per_stn + cell_list[...] % per_stn
    )
    live = lax.broadcasted_iota(jnp.int32, (1, slots), 1) < filled
    station_hot = lax.broadcasted_iota(jnp.int32, (station_total, slots), 0) == station_id
    cell_hot = (lax.broadcasted_iota(jnp.int32, (cell_total, slots), 0) == cell_id) & live
    count = multiply(cell_hot.astype(F32).astype(BF16), station_hot.astype(F32).astype(BF16), NT)
    wide = (station_total, station_total * STATIONS)
    spread = lax.broadcasted_iota(jnp.int32, wide, 0) == (
        lax.broadcasted_iota(jnp.int32, wide, 1) // STATIONS
    )
    return multiply(count.astype(BF16), spread.astype(F32).astype(BF16))


def forward_kernel(station_pieces, cell_pieces, keep, filled, *refs):
    lists_here, refs = refs[:3], refs[3:]
    station_refs = refs[:station_pieces]
    refs = refs[station_pieces:]
    cell_refs = refs[:cell_pieces]
    image, count, station, cell, *outs = refs[cell_pieces:]
    kept = outs[:2] if keep else None
    station_rows, cell_rows, left, right, source, narrow, moments, dense, *held, arrived = outs[
        2 if keep else 0 :
    ]
    copies = [
        pltpu.make_async_copy(here, there, arrived.at[at])
        for at, (here, there) in enumerate(zip(lists_here, held))
    ]
    for copy in copies:
        copy.start()
    station_list, cell_list, residual = held
    width, extent = station.shape[1], cell.shape[1]
    join(cell, cell_refs, 4)
    join(station, station_refs, 3 if keep else 9)
    fill_station_rows(station_rows, station[0:3, :])
    right[...] = station_rows[...].astype(BF16)
    fill_cell_rows(cell_rows, cell[0:3, :])
    transpose_into(left, cell_rows)
    value = cell[3:4, :]
    x, y, z = cell[0:1, :], cell[1:2, :], cell[2:3, :]
    vx, vy, vz = value * x, value * y, value * z
    products = (value, vx, vy, vz, vx * x, vx * y, vx * z, vy * y, vy * z, vz * z)
    for at, row in enumerate(products):
        cell_rows[at : at + 1, :] = row
    cell_rows[10:16, :] = jnp.zeros((6, extent), F32)
    parts = three_parts(cell_rows[0:16, :])
    source[...] = jnp.concatenate([part.astype(BF16) for part in parts], axis=0)
    high, low, unit = narrow_parts(cell_rows[0:16, :])
    narrow[...] = jnp.concatenate([high, low], axis=0).astype(F8)
    spans = width // SPAN

    def turn(which, carry):
        group = which // spans
        lanes = pl.ds(pl.multiple_of(which % spans * SPAN, SPAN), SPAN)
        cells = pl.ds(pl.multiple_of(group * TURN, TURN), TURN)
        squared = multiply(left[cells, :], right[:, lanes])
        high, low = falloff_parts(squared, F8)
        if keep:
            kept[0][cells, lanes] = high
            kept[1][cells, lanes] = low
        for at in range(TURN // CELLS):
            block = group * (TURN // CELLS) + at
            here = pl.ds(pl.multiple_of(block * CELLS, CELLS), CELLS)
            rows = slice(at * CELLS, (at + 1) * CELLS)
            wide = multiply(source[:, here], high[rows])
            fine = multiply(narrow[:, here], low[rows])
            total = wide[0:16] + wide[16:32] + wide[32:48]
            total = total + (fine[0:16] + fine[16:32] * (1.0 / 16.0)) * unit
            moments[block, :, lanes] = total
        return carry

    lax.fori_loop(0, spans * (extent // TURN), turn, 0)
    for copy in copies:
        copy.wait()
    count[...] = listed_counts(
        station_list,
        cell_list,
        filled[0, 0],
        (lax.axis_index("cell") if keep else 0, lax.axis_index("stn")),
        (width // STATIONS, extent // CELLS),
        (residual.shape[1] // STATIONS, extent // CELLS // lax.axis_size("stn")),
    )
    sums = moments[0] * count[0:1, :]
    for block in range(1, extent // CELLS):
        sums = sums + moments[block] * count[block : block + 1, :]
    moments[0] = sums
    rows = width // 128
    for k in range(10):
        pack(dense, k * rows, moments[0, k : k + 1, :])
    for k in range(3):
        pack(dense, (10 + k) * rows, station[k : k + 1, :])
    total, mx, my, mz, mxx, mxy, mxz, myy, myz, mzz, sx, sy, sz = (
        dense[k * rows : (k + 1) * rows, :] for k in range(13)
    )
    xx = sx * (sx * total - 2.0 * mx) + mxx
    yy = sy * (sy * total - 2.0 * my) + myy
    zz = sz * (sz * total - 2.0 * mz) + mzz
    xy = sx * (sy * total - my) - sy * mx + mxy
    xz = sx * (sz * total - mz) - sz * mx + mxz
    yz = sy * (sz * total - mz) - sz * my + myz
    parts = (2.0 * xx - yy - zz, 3.0 * xy, 3.0 * xz, 2.0 * yy - xx - zz, 3.0 * yz)
    for k, part in enumerate(parts):
        image[k * rows : (k + 1) * rows, :] = GROWN * part
    if keep:
        for k in range(6):
            at = 5 * rows + k * (residual.shape[1] // 128)
            pack(image, at, residual[k : k + 1, :])


def tree(values):
    values = list(values)
    while len(values) > 1:
        values = [values[k] + values[k + 1] for k in range(0, len(values), 2)]
    return values[0]


def gather_images(image, residual, image_refs, own):
    width = image.shape[1]
    rows, each = width // 128, own // 128
    norms = []
    for owner in range(width // own):
        blocks = []
        for k in range(5):
            blocks.append(
                tree(
                    ref[k * rows + (owner ^ other) * each : k * rows + ((owner ^ other) + 1) * each, :]
                    for other, ref in enumerate(image_refs)
                )
            )
        blocks.append(-(blocks[0] + blocks[3]))
        squares = 0.0
        for k, block in enumerate(blocks):
            unpack(image, k, owner * own, block)
            squares = squares + block * block
        norms.append(jnp.sum(squares))
    if residual is not None:
        for other, ref in enumerate(image_refs):
            for k in range(6):
                first = 5 * rows + k * each
                unpack(residual, k, other * own, ref[first : first + each, :])
    return tree(norms)


def fill_vectors(vectors, station, residual, image):
    sx, sy, sz = station[0:1, :], station[1:2, :], station[2:3, :]
    for first, source, offset in ((0, *residual), (10, *image)):
        r = [GROWN * source[offset + k : offset + k + 1, :] for k in range(6)]
        axx, ayy, azz = 2.0 * r[0] - r[3] - r[5], 2.0 * r[3] - r[0] - r[5], 2.0 * r[5] - r[0] - r[3]
        axy, axz, ayz = 3.0 * r[1], 3.0 * r[2], 3.0 * r[4]
        whole = (
            sx * (axx * sx + axy * sy + axz * sz) + sy * (ayy * sy + ayz * sz) + azz * sz * sz
        )
        bx = 2.0 * axx * sx + axy * sy + axz * sz
        by = 2.0 * ayy * sy + axy * sx + ayz * sz
        bz = 2.0 * azz * sz + axz * sx + ayz * sy
        for k, row in enumerate((whole, bx, by, bz, axx, axy, axz, ayy, ayz, azz)):
            vectors[first + k : first + k + 1, :] = row
    vectors[20:24, :] = jnp.zeros((4, vectors.shape[1]), F32)


def start_partial(partial, norm):
    side = partial.shape[1] - CELLS
    partial[:, CELLS:] = jnp.full((partial.shape[0], side), norm, F32)


def write_partial(partial, sums, place, block, blocks):
    x, y, z = place[0:1], place[1:2], place[2:3]
    for vector in range(2):
        whole, bx, by, bz, axx, axy, axz, ayy, ayz, azz = (
            sums[10 * vector + k : 10 * vector + k + 1] for k in range(10)
        )
        value = (
            whole
            + x * (x * axx + y * axy + z * axz - bx)
            + y * (y * ayy + z * ayz - by)
            + z * (z * azz - bz)
        )
        partial[pl.ds(vector * blocks + block, 1), 0:CELLS] = value


def kept_adjoint_kernel(count, station, cell, high, low, *refs):
    *image_refs, partial, own_image, image, residual, vectors = refs
    extent, own = cell.shape[1], own_image.shape[1]
    norm = gather_images(image, residual, image_refs, own)
    own_image[...] = image[:, 0:own]
    fill_vectors(vectors, station, (residual, 0), (image, 0))
    start_partial(partial, norm)
    blocks = extent // CELLS

    def turn(group, carry):
        for at in range(BLOCKS_A_TURN):
            block = group * BLOCKS_A_TURN + at
            cells = pl.ds(pl.multiple_of(block * CELLS, CELLS), CELLS)
            counted = vectors[...] * count[pl.ds(block, 1), :]
            weights = jnp.concatenate(three_parts(counted), axis=0).astype(BF16)
            above, below, unit = narrow_parts(counted)
            narrow = jnp.concatenate([above, below], axis=0).astype(F8)
            wide = multiply(high[cells, :], weights, NT).T
            fine = multiply(low[cells, :], narrow, NT).T
            sums = wide[0:24] + wide[24:48] + wide[48:72]
            sums = sums + (fine[0:24] + fine[24:48] * (1.0 / 16.0)) * unit
            write_partial(partial, sums, cell[0:3, cells], block, blocks)
        return carry

    lax.fori_loop(0, blocks // BLOCKS_A_TURN, turn, 0)


def adjoint_kernel(count, station, cell, image_ref, *refs):
    partial, own_image, image, station_rows, cell_rows, left, right, vectors = refs
    width, extent = station.shape[1], cell.shape[1]
    norm = gather_images(image, None, [image_ref], CELLS)
    own_image[...] = image[...]
    fill_cell_rows(cell_rows, cell[0:3, :])
    right[...] = cell_rows[...].astype(BF16)
    fill_station_rows(station_rows, station[0:3, :])
    transpose_into(left, station_rows)
    fill_vectors(vectors, station, (station, 3), (image, 0))
    start_partial(partial, norm)
    blocks = extent // CELLS

    def turn(block, carry):
        cells = pl.ds(pl.multiple_of(block * CELLS, CELLS), CELLS)

        def span_turn(which, sums):
            lanes = pl.ds(pl.multiple_of(which * SPAN, SPAN), SPAN)
            squared = multiply(left[lanes, :], right[:, cells])
            high, low = falloff_parts(squared, BF16)
            parts = three_parts(vectors[:, lanes] * count[pl.ds(block, 1), lanes])
            weights = jnp.concatenate(parts, axis=0).astype(BF16)
            total = multiply(weights, high) + multiply(weights, low)
            return sums + (total[0:24] + total[24:48] + total[48:72])

        sums = lax.fori_loop(0, width // SPAN, span_turn, jnp.zeros((24, CELLS), F32))
        write_partial(partial, sums, cell[0:3, cells], block, blocks)
        return carry

    lax.fori_loop(0, blocks, turn, 0)


def update_kernel(pieces, gradient_norm, densities, direction, residual, image, *refs):
    partial_refs = refs[:pieces]
    densities_next, residual_next, gradient, norm = refs[pieces:]
    blocks = partial_refs[0].shape[0] // 2
    each = blocks // pieces
    step = gradient_norm[0] / tree(ref[0:1, CELLS : CELLS + 1] for ref in partial_refs)
    sums = []
    for k in range(pieces):
        both = [
            tree(
                partial_refs[other][
                    vector * blocks + (k ^ other) * each : vector * blocks + ((k ^ other) + 1) * each,
                    0:CELLS,
                ]
                for other in range(pieces)
            )
            for vector in range(2)
        ]
        block = both[0] - step * both[1]
        sums.append(jnp.sum(block * block, axis=(0, 1), keepdims=True))
        if k == 0:
            for b in range(each):
                pack(gradient, b * (CELLS // 128), block[b : b + 1, :])
    norm[...] = jnp.broadcast_to(tree(sums), norm.shape)
    densities_next[...] = densities[...] + step * direction[...]
    residual_next[...] = residual[...] - step * image[0:6, :]


def finish_kernel(gradient_norm, gradient, direction, *refs):
    *norms, direction_next, norm_next = refs
    total = tree(ref[...] for ref in norms)
    direction_next[...] = gradient[...] + total / gradient_norm[0] * direction[...]
    norm_next[0] = total[0, 0]


def sent(value, axis, size, other):
    return lax.ppermute(value, axis, [(rank, rank ^ other) for rank in range(size)])


def doubled(value, axis, size):
    step = 1
    while step < size // 2:
        value = jnp.concatenate([value, sent(value, axis, size, step)], axis=1)
        step *= 2
    return [value, sent(value, axis, size, step)]


def exchanged(value, axis, size):
    return [value] + [sent(value, axis, size, other) for other in range(1, size)]


def on_device(
    densities,
    residual,
    direction,
    gradient_norm,
    station_place,
    cell_place,
    station_blocks,
    cell_blocks,
    pair_count,
):
    cell_size, stn_size = lax.axis_size("cell"), lax.axis_size("stn")
    direct = cell_size <= 4
    own, cell_own = station_place.shape[1], cell_place.shape[1]
    width, extent = cell_size * own, stn_size * cell_own
    rows, blocks = width // 128, extent // CELLS
    if direct:
        station_parts = doubled(station_place, "cell", cell_size)
    else:
        both = jnp.concatenate([station_place, residual], axis=0)
        station_parts = [lax.all_gather(both, "cell", axis=1, tiled=True)]
    cell_mine = jnp.concatenate([cell_place, direction[None]], axis=0)
    cell_parts = exchanged(cell_mine, "stn", stn_size)
    in_vmem, in_smem = pl.BlockSpec(memory_space=pltpu.VMEM), pl.BlockSpec(memory_space=pltpu.SMEM)
    in_hbm = pl.BlockSpec(memory_space=pltpu.HBM)
    lists = (station_blocks.reshape(1, -1), cell_blocks.reshape(1, -1), residual)
    params = pltpu.CompilerParams(vmem_limit_bytes=(16 if direct else 56) * 2**20)
    small = pltpu.CompilerParams(vmem_limit_bytes=2**20)
    counts = (len(station_parts), len(cell_parts))
    pieces = sum(counts)

    def forward(*refs):
        forward_kernel(*counts, direct, *refs)

    out_shape = [
        jax.ShapeDtypeStruct((5 * rows + (6 * own // 128 if direct else 0), 128), F32),
        jax.ShapeDtypeStruct((blocks, width), F32),
        jax.ShapeDtypeStruct((16, width), F32),
        jax.ShapeDtypeStruct((8, extent), F32),
    ]
    if direct:
        out_shape += [
            jax.ShapeDtypeStruct((extent, width), BF16),
            jax.ShapeDtypeStruct((extent, width), F8),
        ]
    image_part, *kept = pl.pallas_call(
        forward,
        out_shape=out_shape,
        in_specs=[in_smem] + [in_hbm] * 3 + [in_vmem] * pieces,
        out_specs=[in_vmem] * len(out_shape),
        scratch_shapes=[
            pltpu.VMEM((DEPTH, width), F32),
            pltpu.VMEM((DEPTH, extent), F32),
            pltpu.VMEM((extent, DEPTH), BF16),
            pltpu.VMEM((DEPTH, width), BF16),
            pltpu.VMEM((48, extent), BF16),
            pltpu.VMEM((32, extent), F8),
            pltpu.VMEM((blocks, 16, width), F32),
            pltpu.VMEM((13 * rows, 128), F32),
            *(pltpu.VMEM(here.shape, here.dtype) for here in lists),
            pltpu.SemaphoreType.DMA((3,)),
        ],
        compiler_params=params,
        name="forward",
    )(
        pair_count,
        *(pltpu.with_memory_space_constraint(here, pltpu.HBM) for here in lists),
        *station_parts,
        *cell_parts,
    )
    if direct:
        image_parts = exchanged(image_part, "cell", cell_size)
    else:
        image_parts = [lax.psum(image_part, "cell")]

    def adjoint(*refs):
        (kept_adjoint_kernel if direct else adjoint_kernel)(*refs)

    if direct:
        scratch = [pltpu.VMEM((8, width), F32)]
    else:
        scratch = [
            pltpu.VMEM((DEPTH, width), F32),
            pltpu.VMEM((DEPTH, extent), F32),
            pltpu.VMEM((width, DEPTH), BF16),
            pltpu.VMEM((DEPTH, extent), BF16),
        ]
    partial, image_own = pl.pallas_call(
        adjoint,
        out_shape=(
            jax.ShapeDtypeStruct((2 * blocks, CELLS + 128), F32),
            jax.ShapeDtypeStruct((8, own if direct else width), F32),
        ),
        in_specs=[in_vmem] * (len(kept) + len(image_parts)),
        out_specs=(in_vmem, in_vmem),
        scratch_shapes=[
            pltpu.VMEM((8, width), F32),
            *scratch,
            pltpu.VMEM((24, width), F32),
        ],
        compiler_params=params,
        name="adjoint",
    )(*kept, *image_parts)
    if not direct:
        image_own = lax.dynamic_slice_in_dim(image_own, lax.axis_index("cell") * own, own, axis=1)
    partial_parts = exchanged(partial, "stn", stn_size)

    def update(*refs):
        update_kernel(stn_size, *refs)

    flat = direction.reshape(-1, 128)
    densities_next, residual_next, gradient, norm_part = pl.pallas_call(
        update,
        out_shape=(
            jax.ShapeDtypeStruct(flat.shape, F32),
            jax.ShapeDtypeStruct(residual.shape, F32),
            jax.ShapeDtypeStruct(flat.shape, F32),
            jax.ShapeDtypeStruct((1, 128), F32),
        ),
        in_specs=[in_smem] + [in_vmem] * (4 + stn_size),
        out_specs=(in_vmem,) * 4,
        compiler_params=small,
        name="update",
    )(gradient_norm, densities.reshape(flat.shape), flat, residual, image_own, *partial_parts)
    if direct:
        norm_parts = exchanged(norm_part, "cell", cell_size)
    else:
        norm_parts = [lax.psum(norm_part, "cell")]
    direction_next, norm_next = pl.pallas_call(
        finish_kernel,
        out_shape=(
            jax.ShapeDtypeStruct(flat.shape, F32),
            jax.ShapeDtypeStruct((1,), F32),
        ),
        in_specs=[in_smem] + [in_vmem] * (2 + len(norm_parts)),
        out_specs=(in_vmem, in_smem),
        compiler_params=small,
        name="finish",
    )(gradient_norm, gradient, flat, *norm_parts)
    return (densities_next.reshape(-1), residual_next, direction_next.reshape(-1), norm_next)


def solution(mesh):
    in_specs = (
        P(("survey", "cell", "stn")),
        P(None, ("survey", "cell", "stn")),
        P(("survey", "cell", "stn")),
        P("survey"),
        P(None, ("survey", "cell", "stn")),
        P(None, ("survey", "cell", "stn")),
        P(("survey", "cell"), "stn", None),
        P(("survey", "cell"), "stn", None),
        P(("survey", "cell"), "stn"),
    )
    out_specs = (
        P(("survey", "cell", "stn")),
        P(None, ("survey", "cell", "stn")),
        P(("survey", "cell", "stn")),
        P("survey"),
    )
    return jax.shard_map(
        on_device, mesh=mesh, in_specs=in_specs, out_specs=out_specs, check_vma=False
    )
```

```python
import jax
import jax.numpy as jnp
from jax import lax
from jax.experimental import pallas as pl
from jax.experimental.pallas import tpu as pltpu
from jax.sharding import PartitionSpec as P

STATIONS = 128
CELLS = 512
SPAN = 2048
DEPTH = 32
STRENGTH = 0.1
SHRINK = 2.0**-6
GROWN = 2.0**-15 * STRENGTH
TURN = 1024
BLOCKS_A_TURN = 8
F8_TOP = 256.0
F32 = jnp.float32
BF16 = jnp.bfloat16
F8 = jnp.float8_e4m3fn
NN = (((1,), (0,)), ((), ()))
NT = (((1,), (1,)), ((), ()))


def rounded(value):
    return value.astype(BF16).astype(F32)


def three_parts(value):
    high = rounded(value)
    middle = rounded(value - high)
    return high, middle, value - high - middle


def multiply(left, right, numbers=NN):
    return lax.dot_general(left, right, numbers, preferred_element_type=F32)


def falloff_parts(squared, low_type):
    root = lax.rsqrt(squared)
    second = root * root
    falloff = second * second * root
    high = falloff.astype(BF16)
    return high, (falloff - high.astype(F32)).astype(low_type)


def narrow_parts(value):
    top = jnp.maximum(jnp.max(jnp.abs(value), axis=1, keepdims=True), 1e-30)
    scaled = value * (F8_TOP / top)
    high = scaled.astype(F8).astype(F32)
    return high, (scaled - high) * 16.0, top * (1.0 / F8_TOP)


def square_sum(place):
    return place[0:1] * place[0:1] + place[1:2] * place[1:2] + place[2:3] * place[2:3]


def fill_station_rows(rows, place):
    high, middle, low = three_parts(place)
    norms = three_parts(square_sum(place))
    ones = jnp.ones_like(norms[0])
    for at, part in enumerate((high, high, middle, middle, high, low)):
        rows[3 * at : 3 * at + 3, :] = part
    for at, part in enumerate((*norms, ones, ones, ones)):
        rows[18 + at : 19 + at, :] = part
    rows[24:DEPTH, :] = jnp.zeros((DEPTH - 24, place.shape[1]), F32)


def fill_cell_rows(rows, place):
    high, middle, low = three_parts((-2.0 * SHRINK) * place)
    norms = three_parts(SHRINK * square_sum(place))
    ones = jnp.full_like(norms[0], SHRINK)
    for at, part in enumerate((high, middle, high, middle, low, high)):
        rows[3 * at : 3 * at + 3, :] = part
    for at, part in enumerate((ones, ones, ones, *norms)):
        rows[18 + at : 19 + at, :] = part
    rows[24:DEPTH, :] = jnp.zeros((DEPTH - 24, place.shape[1]), F32)


def join(target, pieces, rows):
    at = 0
    for piece in pieces:
        width = piece.shape[1]
        target[0:rows, at : at + width] = piece[0:rows, :]
        at += width


def transpose_into(target, rows):
    for at in range(0, rows.shape[1], 512):
        target[at : at + 512, :] = rows[:, at : at + 512].T.astype(BF16)


def pack(target, base, row):
    for at in range(row.shape[1] // 128):
        target[base + at : base + at + 1, :] = row[:, at * 128 : (at + 1) * 128]


def unpack(target, row, lane, source):
    for at in range(source.shape[0]):
        start = lane + at * 128
        target[row : row + 1, start : start + 128] = source[at : at + 1, :]


def listed_counts(station_list, cell_list, filled, ranks, blocks, own_blocks):
    slots = station_list.shape[1]
    station_total, cell_total = blocks
    per_cell, per_stn = own_blocks
    station_id = (
        lax.bitwise_xor(station_list[...] // per_cell, ranks[0]) * per_cell
        + station_list[...] % per_cell
    )
    cell_id = (
        lax.bitwise_xor(cell_list[...] // per_stn, ranks[1]) * per_stn + cell_list[...] % per_stn
    )
    live = lax.broadcasted_iota(jnp.int32, (1, slots), 1) < filled
    station_hot = lax.broadcasted_iota(jnp.int32, (station_total, slots), 0) == station_id
    cell_hot = (lax.broadcasted_iota(jnp.int32, (cell_total, slots), 0) == cell_id) & live
    count = multiply(cell_hot.astype(F32).astype(BF16), station_hot.astype(F32).astype(BF16), NT)
    wide = (station_total, station_total * STATIONS)
    spread = lax.broadcasted_iota(jnp.int32, wide, 0) == (
        lax.broadcasted_iota(jnp.int32, wide, 1) // STATIONS
    )
    return multiply(count.astype(BF16), spread.astype(F32).astype(BF16))


def prepare_kernel(cell_pieces, keep, scalars, *refs):
    lists_here, cell_refs, refs = refs[:3], refs[3 : 3 + cell_pieces], refs[3 + cell_pieces :]
    cell, count, last_norm, left, source, narrow, units, packed, cell_rows, *held, arrived = refs
    copies = [
        pltpu.make_async_copy(here, there, arrived.at[at])
        for at, (here, there) in enumerate(zip(lists_here, held))
    ]
    for copy in copies:
        copy.start()
    station_list, cell_list, residual = held
    width, extent = count.shape[1], cell.shape[1]
    join(cell, cell_refs, 4)
    fill_cell_rows(cell_rows, cell[0:3, :])
    transpose_into(left, cell_rows)
    value = cell[3:4, :]
    x, y, z = cell[0:1, :], cell[1:2, :], cell[2:3, :]
    vx, vy, vz = value * x, value * y, value * z
    products = (value, vx, vy, vz, vx * x, vx * y, vx * z, vy * y, vy * z, vz * z)
    for at, row in enumerate(products):
        cell_rows[at : at + 1, :] = row
    cell_rows[10:16, :] = jnp.zeros((6, extent), F32)
    parts = three_parts(cell_rows[0:16, :])
    source[...] = jnp.concatenate([part.astype(BF16) for part in parts], axis=0)
    high, low, unit = narrow_parts(cell_rows[0:16, :])
    narrow[...] = jnp.concatenate([high, low], axis=0).astype(F8)
    units[...] = jnp.broadcast_to(unit, units.shape)
    last_norm[...] = scalars[3:4, scalars.shape[1] - 128 :]
    for copy in copies:
        copy.wait()
    count[...] = listed_counts(
        station_list,
        cell_list,
        scalars[3:4, 0:1].astype(jnp.int32),
        (lax.axis_index("cell") if keep else 0, lax.axis_index("stn")),
        (width // STATIONS, extent // CELLS),
        (residual.shape[1] // STATIONS, extent // CELLS // lax.axis_size("stn")),
    )
    for k in range(6):
        pack(packed, k * (residual.shape[1] // 128), residual[k : k + 1, :])


def forward_kernel(station_pieces, keep, count, left, source, narrow, units, packed, *refs):
    station_refs = refs[:station_pieces]
    image, station, *outs = refs[station_pieces:]
    kept = outs[:2] if keep else None
    station_rows, right, moments, dense = outs[2 if keep else 0 :]
    width, extent = station.shape[1], left.shape[0]
    join(station, station_refs, 3 if keep else 9)
    fill_station_rows(station_rows, station[0:3, :])
    right[...] = station_rows[...].astype(BF16)
    unit = units[:, 0:1]
    spans = width // SPAN

    def turn(which, carry):
        group = which // spans
        lanes = pl.ds(pl.multiple_of(which % spans * SPAN, SPAN), SPAN)
        cells = pl.ds(pl.multiple_of(group * TURN, TURN), TURN)
        squared = multiply(left[cells, :], right[:, lanes])
        high, low = falloff_parts(squared, F8)
        if keep:
            kept[0][cells, lanes] = high
            kept[1][cells, lanes] = low
        for at in range(TURN // CELLS):
            block = group * (TURN // CELLS) + at
            here = pl.ds(pl.multiple_of(block * CELLS, CELLS), CELLS)
            rows = slice(at * CELLS, (at + 1) * CELLS)
            wide = multiply(source[:, here], high[rows])
            fine = multiply(narrow[:, here], low[rows])
            total = wide[0:16] + wide[16:32] + wide[32:48]
            total = total + (fine[0:16] + fine[16:32] * (1.0 / 16.0)) * unit
            moments[block, :, lanes] = total
        return carry

    lax.fori_loop(0, spans * (extent // TURN), turn, 0)
    sums = moments[0] * count[0:1, :]
    for block in range(1, extent // CELLS):
        sums = sums + moments[block] * count[block : block + 1, :]
    moments[0] = sums
    rows = width // 128
    for k in range(10):
        pack(dense, k * rows, moments[0, k : k + 1, :])
    for k in range(3):
        pack(dense, (10 + k) * rows, station[k : k + 1, :])
    total, mx, my, mz, mxx, mxy, mxz, myy, myz, mzz, sx, sy, sz = (
        dense[k * rows : (k + 1) * rows, :] for k in range(13)
    )
    xx = sx * (sx * total - 2.0 * mx) + mxx
    yy = sy * (sy * total - 2.0 * my) + myy
    zz = sz * (sz * total - 2.0 * mz) + mzz
    xy = sx * (sy * total - my) - sy * mx + mxy
    xz = sx * (sz * total - mz) - sz * mx + mxz
    yz = sy * (sz * total - mz) - sz * my + myz
    parts = (2.0 * xx - yy - zz, 3.0 * xy, 3.0 * xz, 2.0 * yy - xx - zz, 3.0 * yz)
    for k, part in enumerate(parts):
        image[k * rows : (k + 1) * rows, :] = GROWN * part
    if keep:
        image[5 * rows :, :] = packed[...]


def tree(values):
    values = list(values)
    while len(values) > 1:
        values = [values[k] + values[k + 1] for k in range(0, len(values), 2)]
    return values[0]


def gather_images(image, residual, image_refs, own):
    width = image.shape[1]
    rows, each = width // 128, own // 128
    norms = []
    for owner in range(width // own):
        blocks = []
        for k in range(5):
            blocks.append(
                tree(
                    ref[k * rows + (owner ^ other) * each : k * rows + ((owner ^ other) + 1) * each, :]
                    for other, ref in enumerate(image_refs)
                )
            )
        blocks.append(-(blocks[0] + blocks[3]))
        squares = 0.0
        for k, block in enumerate(blocks):
            unpack(image, k, owner * own, block)
            squares = squares + block * block
        norms.append(jnp.sum(squares))
    if residual is not None:
        for other, ref in enumerate(image_refs):
            for k in range(6):
                first = 5 * rows + k * each
                unpack(residual, k, other * own, ref[first : first + each, :])
    return tree(norms)


def fill_vectors(vectors, station, residual, image):
    sx, sy, sz = station[0:1, :], station[1:2, :], station[2:3, :]
    for first, source, offset in ((0, *residual), (10, *image)):
        r = [GROWN * source[offset + k : offset + k + 1, :] for k in range(6)]
        axx, ayy, azz = 2.0 * r[0] - r[3] - r[5], 2.0 * r[3] - r[0] - r[5], 2.0 * r[5] - r[0] - r[3]
        axy, axz, ayz = 3.0 * r[1], 3.0 * r[2], 3.0 * r[4]
        whole = (
            sx * (axx * sx + axy * sy + axz * sz) + sy * (ayy * sy + ayz * sz) + azz * sz * sz
        )
        bx = 2.0 * axx * sx + axy * sy + axz * sz
        by = 2.0 * ayy * sy + axy * sx + ayz * sz
        bz = 2.0 * azz * sz + axz * sx + ayz * sy
        for k, row in enumerate((whole, bx, by, bz, axx, axy, axz, ayy, ayz, azz)):
            vectors[first + k : first + k + 1, :] = row
    vectors[20:24, :] = jnp.zeros((4, vectors.shape[1]), F32)


def start_partial(partial, norm):
    side = partial.shape[1] - CELLS
    partial[:, CELLS:] = jnp.full((partial.shape[0], side), norm, F32)


def write_partial(partial, sums, place, block, blocks):
    x, y, z = place[0:1], place[1:2], place[2:3]
    for vector in range(2):
        whole, bx, by, bz, axx, axy, axz, ayy, ayz, azz = (
            sums[10 * vector + k : 10 * vector + k + 1] for k in range(10)
        )
        value = (
            whole
            + x * (x * axx + y * axy + z * axz - bx)
            + y * (y * ayy + z * ayz - by)
            + z * (z * azz - bz)
        )
        partial[pl.ds(vector * blocks + block, 1), 0:CELLS] = value


def kept_adjoint_kernel(count, station, cell, high, low, *refs):
    *image_refs, partial, own_image, image, residual, vectors = refs
    extent, own = cell.shape[1], own_image.shape[1]
    norm = gather_images(image, residual, image_refs, own)
    own_image[...] = image[:, 0:own]
    fill_vectors(vectors, station, (residual, 0), (image, 0))
    start_partial(partial, norm)
    blocks = extent // CELLS

    def turn(group, carry):
        for at in range(BLOCKS_A_TURN):
            block = group * BLOCKS_A_TURN + at
            cells = pl.ds(pl.multiple_of(block * CELLS, CELLS), CELLS)
            counted = vectors[...] * count[pl.ds(block, 1), :]
            weights = jnp.concatenate(three_parts(counted), axis=0).astype(BF16)
            above, below, unit = narrow_parts(counted)
            narrow = jnp.concatenate([above, below], axis=0).astype(F8)
            wide = multiply(high[cells, :], weights, NT).T
            fine = multiply(low[cells, :], narrow, NT).T
            sums = wide[0:24] + wide[24:48] + wide[48:72]
            sums = sums + (fine[0:24] + fine[24:48] * (1.0 / 16.0)) * unit
            write_partial(partial, sums, cell[0:3, cells], block, blocks)
        return carry

    lax.fori_loop(0, blocks // BLOCKS_A_TURN, turn, 0)


def adjoint_kernel(count, station, cell, image_ref, *refs):
    partial, own_image, image, station_rows, cell_rows, left, right, vectors = refs
    width, extent = station.shape[1], cell.shape[1]
    norm = gather_images(image, None, [image_ref], CELLS)
    own_image[...] = image[...]
    fill_cell_rows(cell_rows, cell[0:3, :])
    right[...] = cell_rows[...].astype(BF16)
    fill_station_rows(station_rows, station[0:3, :])
    transpose_into(left, station_rows)
    fill_vectors(vectors, station, (station, 3), (image, 0))
    start_partial(partial, norm)
    blocks = extent // CELLS

    def turn(block, carry):
        cells = pl.ds(pl.multiple_of(block * CELLS, CELLS), CELLS)

        def span_turn(which, sums):
            lanes = pl.ds(pl.multiple_of(which * SPAN, SPAN), SPAN)
            squared = multiply(left[lanes, :], right[:, cells])
            high, low = falloff_parts(squared, BF16)
            parts = three_parts(vectors[:, lanes] * count[pl.ds(block, 1), lanes])
            weights = jnp.concatenate(parts, axis=0).astype(BF16)
            total = multiply(weights, high) + multiply(weights, low)
            return sums + (total[0:24] + total[24:48] + total[48:72])

        sums = lax.fori_loop(0, width // SPAN, span_turn, jnp.zeros((24, CELLS), F32))
        write_partial(partial, sums, cell[0:3, cells], block, blocks)
        return carry

    lax.fori_loop(0, blocks, turn, 0)


def update_kernel(pieces, gradient_norm, densities, direction, residual, image, *refs):
    partial_refs = refs[:pieces]
    densities_next, residual_next, gradient, norm = refs[pieces:]
    blocks = partial_refs[0].shape[0] // 2
    each = blocks // pieces
    step = gradient_norm[0:1, 0:1] / tree(ref[0:1, CELLS : CELLS + 1] for ref in partial_refs)
    sums = []
    for k in range(pieces):
        both = [
            tree(
                partial_refs[other][
                    vector * blocks + (k ^ other) * each : vector * blocks + ((k ^ other) + 1) * each,
                    0:CELLS,
                ]
                for other in range(pieces)
            )
            for vector in range(2)
        ]
        block = both[0] - step * both[1]
        sums.append(jnp.sum(block * block, axis=(0, 1), keepdims=True))
        if k == 0:
            for b in range(each):
                pack(gradient, b * (CELLS // 128), block[b : b + 1, :])
    norm[...] = jnp.broadcast_to(tree(sums), norm.shape)
    densities_next[...] = densities[...] + step * direction[...]
    residual_next[...] = residual[...] - step * image[0:6, :]


def finish_kernel(gradient_norm, gradient, direction, *refs):
    *norms, direction_next, norm_next = refs
    total = tree(ref[...] for ref in norms)
    direction_next[...] = gradient[...] + total / gradient_norm[...] * direction[...]
    norm_next[0] = total[0, 0]


def sent(value, axis, size, other):
    return lax.ppermute(value, axis, [(rank, rank ^ other) for rank in range(size)])


def exchanged(value, axis, size):
    return [value] + [sent(value, axis, size, other) for other in range(1, size)]


def on_device(
    densities,
    residual,
    direction,
    gradient_norm,
    station_place,
    cell_place,
    station_blocks,
    cell_blocks,
    pair_count,
):
    cell_size, stn_size = lax.axis_size("cell"), lax.axis_size("stn")
    direct = cell_size <= 4
    own, cell_own = station_place.shape[1], cell_place.shape[1]
    width, extent = cell_size * own, stn_size * cell_own
    rows, blocks = width // 128, extent // CELLS
    scalar_row = jnp.concatenate(
        [
            jnp.broadcast_to(pair_count.astype(F32), (1, own)),
            jnp.broadcast_to(gradient_norm[None], (1, own)),
        ],
        axis=1,
    )
    if direct:
        near = sent(station_place, "cell", cell_size, 1)
        scalars = jnp.concatenate(
            [jnp.concatenate([station_place, near], axis=1), scalar_row], axis=0
        )
        station_parts = [scalars] + [
            sent(scalars, "cell", cell_size, other) for other in range(2, cell_size, 2)
        ]
    else:
        both = jnp.concatenate([station_place, residual], axis=0)
        station_parts = [lax.all_gather(both, "cell", axis=1, tiled=True)]
        scalars = jnp.concatenate([jnp.zeros((3, 2 * own), F32), scalar_row], axis=0)
    cell_mine = jnp.concatenate([cell_place, direction[None]], axis=0)
    cell_parts = exchanged(cell_mine, "stn", stn_size)
    in_vmem, in_smem = (pl.BlockSpec(memory_space=space) for space in (pltpu.VMEM, pltpu.SMEM))
    in_hbm = pl.BlockSpec(memory_space=pltpu.HBM)
    lists = (station_blocks.reshape(1, -1), cell_blocks.reshape(1, -1), residual)
    params = pltpu.CompilerParams(vmem_limit_bytes=(16 if direct else 56) * 2**20)
    small = pltpu.CompilerParams(vmem_limit_bytes=2**20)

    def prepare(*refs):
        prepare_kernel(len(cell_parts), direct, *refs)

    cell_all, count, last_norm, *prepared = pl.pallas_call(
        prepare,
        out_shape=(
            jax.ShapeDtypeStruct((8, extent), F32),
            jax.ShapeDtypeStruct((blocks, width), F32),
            jax.ShapeDtypeStruct((1, 128), F32),
            jax.ShapeDtypeStruct((extent, DEPTH), BF16),
            jax.ShapeDtypeStruct((48, extent), BF16),
            jax.ShapeDtypeStruct((32, extent), F8),
            jax.ShapeDtypeStruct((16, 128), F32),
            jax.ShapeDtypeStruct((6 * own // 128, 128), F32),
        ),
        in_specs=[in_vmem] + [in_hbm] * 3 + [in_vmem] * len(cell_parts),
        out_specs=(in_vmem,) * 8,
        scratch_shapes=[
            pltpu.VMEM((DEPTH, extent), F32),
            *(pltpu.VMEM(here.shape, here.dtype) for here in lists),
            pltpu.SemaphoreType.DMA((3,)),
        ],
        compiler_params=pltpu.CompilerParams(vmem_limit_bytes=(8 if direct else 56) * 2**20),
        cost_estimate=pl.CostEstimate(flops=2**22, bytes_accessed=2**21, transcendentals=0),
        name="prepare",
    )(
        scalars,
        *(pltpu.with_memory_space_constraint(here, pltpu.HBM) for here in lists),
        *cell_parts,
    )

    def forward(*refs):
        forward_kernel(len(station_parts), direct, *refs)

    out_shape = [
        jax.ShapeDtypeStruct((5 * rows + (6 * own // 128 if direct else 0), 128), F32),
        jax.ShapeDtypeStruct((16, width), F32),
    ]
    if direct:
        out_shape += [
            jax.ShapeDtypeStruct((extent, width), BF16),
            jax.ShapeDtypeStruct((extent, width), F8),
        ]
    image_part, station_all, *kept = pl.pallas_call(
        forward,
        out_shape=out_shape,
        in_specs=[in_vmem] * (1 + len(prepared) + len(station_parts)),
        out_specs=[in_vmem] * len(out_shape),
        scratch_shapes=[
            pltpu.VMEM((DEPTH, width), F32),
            pltpu.VMEM((DEPTH, width), BF16),
            pltpu.VMEM((blocks, 16, width), F32),
            pltpu.VMEM((13 * rows, 128), F32),
        ],
        compiler_params=params,
        name="forward",
    )(count, *prepared, *station_parts)
    if direct:
        image_parts = exchanged(image_part, "cell", cell_size)
    else:
        image_parts = [lax.psum(image_part, "cell")]

    def adjoint(*refs):
        (kept_adjoint_kernel if direct else adjoint_kernel)(*refs)

    if direct:
        scratch = [pltpu.VMEM((8, width), F32)]
    else:
        scratch = [
            pltpu.VMEM((DEPTH, width), F32),
            pltpu.VMEM((DEPTH, extent), F32),
            pltpu.VMEM((width, DEPTH), BF16),
            pltpu.VMEM((DEPTH, extent), BF16),
        ]
    partial, image_own = pl.pallas_call(
        adjoint,
        out_shape=(
            jax.ShapeDtypeStruct((2 * blocks, CELLS + 128), F32),
            jax.ShapeDtypeStruct((8, own if direct else width), F32),
        ),
        in_specs=[in_vmem] * (3 + len(kept) + len(image_parts)),
        out_specs=(in_vmem, in_vmem),
        scratch_shapes=[
            pltpu.VMEM((8, width), F32),
            *scratch,
            pltpu.VMEM((24, width), F32),
        ],
        compiler_params=params,
        name="adjoint",
    )(count, station_all, cell_all, *kept, *image_parts)
    if not direct:
        image_own = lax.dynamic_slice_in_dim(image_own, lax.axis_index("cell") * own, own, axis=1)
    partial_parts = exchanged(partial, "stn", stn_size)

    def update(*refs):
        update_kernel(stn_size, *refs)

    flat = direction.reshape(-1, 128)
    densities_next, residual_next, gradient, norm_part = pl.pallas_call(
        update,
        out_shape=(
            jax.ShapeDtypeStruct(flat.shape, F32),
            jax.ShapeDtypeStruct(residual.shape, F32),
            jax.ShapeDtypeStruct(flat.shape, F32),
            jax.ShapeDtypeStruct((1, 128), F32),
        ),
        in_specs=[in_vmem] * (5 + stn_size),
        out_specs=(in_vmem,) * 4,
        compiler_params=small,
        name="update",
    )(last_norm, densities.reshape(flat.shape), flat, residual, image_own, *partial_parts)
    if direct:
        norm_parts = exchanged(norm_part, "cell", cell_size)
    else:
        norm_parts = [lax.psum(norm_part, "cell")]
    direction_next, norm_next = pl.pallas_call(
        finish_kernel,
        out_shape=(
            jax.ShapeDtypeStruct(flat.shape, F32),
            jax.ShapeDtypeStruct((1,), F32),
        ),
        in_specs=[in_vmem] * (3 + len(norm_parts)),
        out_specs=(in_vmem, in_smem),
        compiler_params=small,
        name="finish",
    )(last_norm, gradient, flat, *norm_parts)
    return (densities_next.reshape(-1), residual_next, direction_next.reshape(-1), norm_next)


def solution(mesh):
    in_specs = (
        P(("survey", "cell", "stn")),
        P(None, ("survey", "cell", "stn")),
        P(("survey", "cell", "stn")),
        P("survey"),
        P(None, ("survey", "cell", "stn")),
        P(None, ("survey", "cell", "stn")),
        P(("survey", "cell"), "stn", None),
        P(("survey", "cell"), "stn", None),
        P(("survey", "cell"), "stn"),
    )
    out_specs = (
        P(("survey", "cell", "stn")),
        P(None, ("survey", "cell", "stn")),
        P(("survey", "cell", "stn")),
        P("survey"),
    )
    return jax.shard_map(
        on_device, mesh=mesh, in_specs=in_specs, out_specs=out_specs, check_vma=False
    )
```

```python
import jax
import jax.numpy as jnp
from jax import lax
from jax.experimental import pallas as pl
from jax.experimental.pallas import tpu as pltpu
from jax.sharding import PartitionSpec as P

STATIONS = 128
CELLS = 512
SPAN = 2048
DEPTH = 32
STRENGTH = 0.1
SHRINK = 2.0**-6
GROWN = 2.0**-15 * STRENGTH
TURN = 1024
BLOCKS_A_TURN = 8
F8_TOP = 256.0
F32 = jnp.float32
BF16 = jnp.bfloat16
F8 = jnp.float8_e4m3fn
NN = (((1,), (0,)), ((), ()))
NT = (((1,), (1,)), ((), ()))


def rounded(value):
    return value.astype(BF16).astype(F32)


def three_parts(value):
    high = rounded(value)
    middle = rounded(value - high)
    return high, middle, value - high - middle


def multiply(left, right, numbers=NN):
    return lax.dot_general(left, right, numbers, preferred_element_type=F32)


def falloff_parts(squared, low_type):
    root = lax.rsqrt(squared)
    second = root * root
    falloff = second * second * root
    high = falloff.astype(BF16)
    return high, (falloff - high.astype(F32)).astype(low_type)


def narrow_parts(value):
    top = jnp.maximum(jnp.max(jnp.abs(value), axis=1, keepdims=True), 1e-30)
    scaled = value * (F8_TOP / top)
    high = scaled.astype(F8).astype(F32)
    return high, (scaled - high) * 16.0, top * (1.0 / F8_TOP)


def square_sum(place):
    return place[0:1] * place[0:1] + place[1:2] * place[1:2] + place[2:3] * place[2:3]


def fill_station_rows(rows, place):
    high, middle, low = three_parts(place)
    norms = three_parts(square_sum(place))
    ones = jnp.ones_like(norms[0])
    for at, part in enumerate((high, high, middle, middle, high, low)):
        rows[3 * at : 3 * at + 3, :] = part
    for at, part in enumerate((*norms, ones, ones, ones)):
        rows[18 + at : 19 + at, :] = part
    rows[24:DEPTH, :] = jnp.zeros((DEPTH - 24, place.shape[1]), F32)


def fill_cell_rows(rows, place):
    high, middle, low = three_parts((-2.0 * SHRINK) * place)
    norms = three_parts(SHRINK * square_sum(place))
    ones = jnp.full_like(norms[0], SHRINK)
    for at, part in enumerate((high, middle, high, middle, low, high)):
        rows[3 * at : 3 * at + 3, :] = part
    for at, part in enumerate((ones, ones, ones, *norms)):
        rows[18 + at : 19 + at, :] = part
    rows[24:DEPTH, :] = jnp.zeros((DEPTH - 24, place.shape[1]), F32)


def join(target, pieces, rows):
    at = 0
    for piece in pieces:
        width = piece.shape[1]
        target[0:rows, at : at + width] = piece[0:rows, :]
        at += width


def transpose_into(target, rows):
    for at in range(0, rows.shape[1], 512):
        target[at : at + 512, :] = rows[:, at : at + 512].T.astype(BF16)


def pack(target, base, row):
    for at in range(row.shape[1] // 128):
        target[base + at : base + at + 1, :] = row[:, at * 128 : (at + 1) * 128]


def unpack(target, row, lane, source):
    for at in range(source.shape[0]):
        start = lane + at * 128
        target[row : row + 1, start : start + 128] = source[at : at + 1, :]


def listed_counts(station_list, cell_list, filled, ranks, blocks, own_blocks):
    slots = station_list.shape[1]
    station_total, cell_total = blocks
    per_cell, per_stn = own_blocks
    station_id = (
        lax.bitwise_xor(station_list[...] // per_cell, ranks[0]) * per_cell
        + station_list[...] % per_cell
    )
    cell_id = (
        lax.bitwise_xor(cell_list[...] // per_stn, ranks[1]) * per_stn + cell_list[...] % per_stn
    )
    live = lax.broadcasted_iota(jnp.int32, (1, slots), 1) < filled
    station_hot = lax.broadcasted_iota(jnp.int32, (station_total, slots), 0) == station_id
    cell_hot = (lax.broadcasted_iota(jnp.int32, (cell_total, slots), 0) == cell_id) & live
    count = multiply(cell_hot.astype(F32).astype(BF16), station_hot.astype(F32).astype(BF16), NT)
    wide = (station_total, station_total * STATIONS)
    spread = lax.broadcasted_iota(jnp.int32, wide, 0) == (
        lax.broadcasted_iota(jnp.int32, wide, 1) // STATIONS
    )
    return multiply(count.astype(BF16), spread.astype(F32).astype(BF16))


def prepare_kernel(cell_pieces, keep, filled, scalars, *refs):
    lists_here, cell_refs, refs = refs[:3], refs[3 : 3 + cell_pieces], refs[3 + cell_pieces :]
    cell, count, last_norm, left, source, narrow, units, packed, cell_rows, *held, arrived = refs
    copies = [
        pltpu.make_async_copy(here, there, arrived.at[at])
        for at, (here, there) in enumerate(zip(lists_here, held))
    ]
    for copy in copies:
        copy.start()
    station_list, cell_list, residual = held
    width, extent = count.shape[1], cell.shape[1]
    join(cell, cell_refs, 4)
    fill_cell_rows(cell_rows, cell[0:3, :])
    transpose_into(left, cell_rows)
    value = cell[3:4, :]
    x, y, z = cell[0:1, :], cell[1:2, :], cell[2:3, :]
    vx, vy, vz = value * x, value * y, value * z
    products = (value, vx, vy, vz, vx * x, vx * y, vx * z, vy * y, vy * z, vz * z)
    for at, row in enumerate(products):
        cell_rows[at : at + 1, :] = row
    cell_rows[10:16, :] = jnp.zeros((6, extent), F32)
    parts = three_parts(cell_rows[0:16, :])
    source[...] = jnp.concatenate([part.astype(BF16) for part in parts], axis=0)
    high, low, unit = narrow_parts(cell_rows[0:16, :])
    narrow[...] = jnp.concatenate([high, low], axis=0).astype(F8)
    units[...] = jnp.broadcast_to(unit, units.shape)
    last_norm[...] = scalars[3:4, scalars.shape[1] - 128 :]
    for copy in copies:
        copy.wait()
    count[...] = listed_counts(
        station_list,
        cell_list,
        filled[0, 0],
        (lax.axis_index("cell") if keep else 0, lax.axis_index("stn")),
        (width // STATIONS, extent // CELLS),
        (residual.shape[1] // STATIONS, extent // CELLS // lax.axis_size("stn")),
    )
    for k in range(6):
        pack(packed, k * (residual.shape[1] // 128), residual[k : k + 1, :])


def forward_kernel(station_pieces, keep, count, left, source, narrow, units, packed, *refs):
    station_refs = refs[:station_pieces]
    image, station, *outs = refs[station_pieces:]
    kept = outs[:2] if keep else None
    station_rows, right, moments, dense = outs[2 if keep else 0 :]
    width, extent = station.shape[1], left.shape[0]
    join(station, station_refs, 3 if keep else 9)
    fill_station_rows(station_rows, station[0:3, :])
    right[...] = station_rows[...].astype(BF16)
    unit = units[:, 0:1]
    spans = width // SPAN

    def turn(which, carry):
        group = which // spans
        lanes = pl.ds(pl.multiple_of(which % spans * SPAN, SPAN), SPAN)
        cells = pl.ds(pl.multiple_of(group * TURN, TURN), TURN)
        squared = multiply(left[cells, :], right[:, lanes])
        high, low = falloff_parts(squared, F8)
        if keep:
            kept[0][cells, lanes] = high
            kept[1][cells, lanes] = low
        for at in range(TURN // CELLS):
            block = group * (TURN // CELLS) + at
            here = pl.ds(pl.multiple_of(block * CELLS, CELLS), CELLS)
            rows = slice(at * CELLS, (at + 1) * CELLS)
            wide = multiply(source[:, here], high[rows])
            fine = multiply(narrow[:, here], low[rows])
            total = wide[0:16] + wide[16:32] + wide[32:48]
            total = total + (fine[0:16] + fine[16:32] * (1.0 / 16.0)) * unit
            moments[block, :, lanes] = total
        return carry

    lax.fori_loop(0, spans * (extent // TURN), turn, 0)
    sums = moments[0] * count[0:1, :]
    for block in range(1, extent // CELLS):
        sums = sums + moments[block] * count[block : block + 1, :]
    moments[0] = sums
    rows = width // 128
    for k in range(10):
        pack(dense, k * rows, moments[0, k : k + 1, :])
    for k in range(3):
        pack(dense, (10 + k) * rows, station[k : k + 1, :])
    total, mx, my, mz, mxx, mxy, mxz, myy, myz, mzz, sx, sy, sz = (
        dense[k * rows : (k + 1) * rows, :] for k in range(13)
    )
    xx = sx * (sx * total - 2.0 * mx) + mxx
    yy = sy * (sy * total - 2.0 * my) + myy
    zz = sz * (sz * total - 2.0 * mz) + mzz
    xy = sx * (sy * total - my) - sy * mx + mxy
    xz = sx * (sz * total - mz) - sz * mx + mxz
    yz = sy * (sz * total - mz) - sz * my + myz
    parts = (2.0 * xx - yy - zz, 3.0 * xy, 3.0 * xz, 2.0 * yy - xx - zz, 3.0 * yz)
    for k, part in enumerate(parts):
        image[k * rows : (k + 1) * rows, :] = GROWN * part
    if keep:
        image[5 * rows :, :] = packed[...]


def tree(values):
    values = list(values)
    while len(values) > 1:
        values = [values[k] + values[k + 1] for k in range(0, len(values), 2)]
    return values[0]


def gather_images(image, residual, image_refs, own):
    width = image.shape[1]
    rows, each = width // 128, own // 128
    norms = []
    for owner in range(width // own):
        blocks = []
        for k in range(5):
            blocks.append(
                tree(
                    ref[k * rows + (owner ^ other) * each : k * rows + ((owner ^ other) + 1) * each, :]
                    for other, ref in enumerate(image_refs)
                )
            )
        blocks.append(-(blocks[0] + blocks[3]))
        squares = 0.0
        for k, block in enumerate(blocks):
            unpack(image, k, owner * own, block)
            squares = squares + block * block
        norms.append(jnp.sum(squares))
    if residual is not None:
        for other, ref in enumerate(image_refs):
            for k in range(6):
                first = 5 * rows + k * each
                unpack(residual, k, other * own, ref[first : first + each, :])
    return tree(norms)


def fill_vectors(vectors, station, residual, image):
    sx, sy, sz = station[0:1, :], station[1:2, :], station[2:3, :]
    for first, source, offset in ((0, *residual), (10, *image)):
        r = [GROWN * source[offset + k : offset + k + 1, :] for k in range(6)]
        axx, ayy, azz = 2.0 * r[0] - r[3] - r[5], 2.0 * r[3] - r[0] - r[5], 2.0 * r[5] - r[0] - r[3]
        axy, axz, ayz = 3.0 * r[1], 3.0 * r[2], 3.0 * r[4]
        whole = (
            sx * (axx * sx + axy * sy + axz * sz) + sy * (ayy * sy + ayz * sz) + azz * sz * sz
        )
        bx = 2.0 * axx * sx + axy * sy + axz * sz
        by = 2.0 * ayy * sy + axy * sx + ayz * sz
        bz = 2.0 * azz * sz + axz * sx + ayz * sy
        for k, row in enumerate((whole, bx, by, bz, axx, axy, axz, ayy, ayz, azz)):
            vectors[first + k : first + k + 1, :] = row
    vectors[20:24, :] = jnp.zeros((4, vectors.shape[1]), F32)


def start_partial(partial, norm):
    side = partial.shape[1] - CELLS
    partial[:, CELLS:] = jnp.full((partial.shape[0], side), norm, F32)


def write_partial(partial, sums, place, block, blocks):
    x, y, z = place[0:1], place[1:2], place[2:3]
    for vector in range(2):
        whole, bx, by, bz, axx, axy, axz, ayy, ayz, azz = (
            sums[10 * vector + k : 10 * vector + k + 1] for k in range(10)
        )
        value = (
            whole
            + x * (x * axx + y * axy + z * axz - bx)
            + y * (y * ayy + z * ayz - by)
            + z * (z * azz - bz)
        )
        partial[pl.ds(vector * blocks + block, 1), 0:CELLS] = value


def kept_adjoint_kernel(count, station, cell, high, low, *refs):
    *image_refs, partial, own_image, image, residual, vectors = refs
    extent, own = cell.shape[1], own_image.shape[1]
    norm = gather_images(image, residual, image_refs, own)
    own_image[...] = image[:, 0:own]
    fill_vectors(vectors, station, (residual, 0), (image, 0))
    start_partial(partial, norm)
    blocks = extent // CELLS

    def turn(group, carry):
        for at in range(BLOCKS_A_TURN):
            block = group * BLOCKS_A_TURN + at
            cells = pl.ds(pl.multiple_of(block * CELLS, CELLS), CELLS)
            counted = vectors[...] * count[pl.ds(block, 1), :]
            weights = jnp.concatenate(three_parts(counted), axis=0).astype(BF16)
            above, below, unit = narrow_parts(counted)
            narrow = jnp.concatenate([above, below], axis=0).astype(F8)
            wide = multiply(high[cells, :], weights, NT).T
            fine = multiply(low[cells, :], narrow, NT).T
            sums = wide[0:24] + wide[24:48] + wide[48:72]
            sums = sums + (fine[0:24] + fine[24:48] * (1.0 / 16.0)) * unit
            write_partial(partial, sums, cell[0:3, cells], block, blocks)
        return carry

    lax.fori_loop(0, blocks // BLOCKS_A_TURN, turn, 0)


def adjoint_kernel(count, station, cell, image_ref, *refs):
    partial, own_image, image, station_rows, cell_rows, left, right, vectors = refs
    width, extent = station.shape[1], cell.shape[1]
    norm = gather_images(image, None, [image_ref], CELLS)
    own_image[...] = image[...]
    fill_cell_rows(cell_rows, cell[0:3, :])
    right[...] = cell_rows[...].astype(BF16)
    fill_station_rows(station_rows, station[0:3, :])
    transpose_into(left, station_rows)
    fill_vectors(vectors, station, (station, 3), (image, 0))
    start_partial(partial, norm)
    blocks = extent // CELLS

    def turn(block, carry):
        cells = pl.ds(pl.multiple_of(block * CELLS, CELLS), CELLS)

        def span_turn(which, sums):
            lanes = pl.ds(pl.multiple_of(which * SPAN, SPAN), SPAN)
            squared = multiply(left[lanes, :], right[:, cells])
            high, low = falloff_parts(squared, BF16)
            parts = three_parts(vectors[:, lanes] * count[pl.ds(block, 1), lanes])
            weights = jnp.concatenate(parts, axis=0).astype(BF16)
            total = multiply(weights, high) + multiply(weights, low)
            return sums + (total[0:24] + total[24:48] + total[48:72])

        sums = lax.fori_loop(0, width // SPAN, span_turn, jnp.zeros((24, CELLS), F32))
        write_partial(partial, sums, cell[0:3, cells], block, blocks)
        return carry

    lax.fori_loop(0, blocks, turn, 0)


def update_kernel(pieces, gradient_norm, densities, direction, residual, image, *refs):
    partial_refs = refs[:pieces]
    densities_next, residual_next, gradient, norm = refs[pieces:]
    blocks = partial_refs[0].shape[0] // 2
    each = blocks // pieces
    step = gradient_norm[0:1, 0:1] / tree(ref[0:1, CELLS : CELLS + 1] for ref in partial_refs)
    sums = []
    for k in range(pieces):
        both = [
            tree(
                partial_refs[other][
                    vector * blocks + (k ^ other) * each : vector * blocks + ((k ^ other) + 1) * each,
                    0:CELLS,
                ]
                for other in range(pieces)
            )
            for vector in range(2)
        ]
        block = both[0] - step * both[1]
        sums.append(jnp.sum(block * block, axis=(0, 1), keepdims=True))
        if k == 0:
            for b in range(each):
                pack(gradient, b * (CELLS // 128), block[b : b + 1, :])
    norm[...] = jnp.broadcast_to(tree(sums), norm.shape)
    densities_next[...] = densities[...] + step * direction[...]
    residual_next[...] = residual[...] - step * image[0:6, :]


def finish_kernel(gradient_norm, gradient, direction, *refs):
    *norms, direction_next, norm_next = refs
    total = tree(ref[...] for ref in norms)
    direction_next[...] = gradient[...] + total / gradient_norm[...] * direction[...]
    norm_next[0] = total[0, 0]


def sent(value, axis, size, other):
    return lax.ppermute(value, axis, [(rank, rank ^ other) for rank in range(size)])


def exchanged(value, axis, size):
    return [value] + [sent(value, axis, size, other) for other in range(1, size)]


def on_device(
    densities,
    residual,
    direction,
    gradient_norm,
    station_place,
    cell_place,
    station_blocks,
    cell_blocks,
    pair_count,
):
    cell_size, stn_size = lax.axis_size("cell"), lax.axis_size("stn")
    direct = cell_size <= 4
    own, cell_own = station_place.shape[1], cell_place.shape[1]
    width, extent = cell_size * own, stn_size * cell_own
    rows, blocks = width // 128, extent // CELLS
    scalar_row = jnp.broadcast_to(gradient_norm[None], (1, 2 * own))
    if direct:
        near = sent(station_place, "cell", cell_size, 1)
        scalars = jnp.concatenate(
            [jnp.concatenate([station_place, near], axis=1), scalar_row], axis=0
        )
        station_parts = [scalars] + [
            sent(scalars, "cell", cell_size, other) for other in range(2, cell_size, 2)
        ]
    else:
        both = jnp.concatenate([station_place, residual], axis=0)
        station_parts = [lax.all_gather(both, "cell", axis=1, tiled=True)]
        scalars = jnp.concatenate([jnp.zeros((3, 2 * own), F32), scalar_row], axis=0)
    cell_mine = jnp.concatenate([cell_place, direction[None]], axis=0)
    cell_parts = exchanged(cell_mine, "stn", stn_size)
    in_vmem, in_smem = (pl.BlockSpec(memory_space=space) for space in (pltpu.VMEM, pltpu.SMEM))
    in_hbm = pl.BlockSpec(memory_space=pltpu.HBM)
    lists = (station_blocks.reshape(1, -1), cell_blocks.reshape(1, -1), residual)
    params = pltpu.CompilerParams(vmem_limit_bytes=(16 if direct else 56) * 2**20)
    small = pltpu.CompilerParams(vmem_limit_bytes=2**20)

    def prepare(*refs):
        prepare_kernel(len(cell_parts), direct, *refs)

    cell_all, count, last_norm, *prepared = pl.pallas_call(
        prepare,
        out_shape=(
            jax.ShapeDtypeStruct((8, extent), F32),
            jax.ShapeDtypeStruct((blocks, width), F32),
            jax.ShapeDtypeStruct((1, 128), F32),
            jax.ShapeDtypeStruct((extent, DEPTH), BF16),
            jax.ShapeDtypeStruct((48, extent), BF16),
            jax.ShapeDtypeStruct((32, extent), F8),
            jax.ShapeDtypeStruct((16, 128), F32),
            jax.ShapeDtypeStruct((6 * own // 128, 128), F32),
        ),
        in_specs=[in_smem, in_vmem] + [in_hbm] * 3 + [in_vmem] * len(cell_parts),
        out_specs=(in_vmem,) * 8,
        scratch_shapes=[
            pltpu.VMEM((DEPTH, extent), F32),
            *(pltpu.VMEM(here.shape, here.dtype) for here in lists),
            pltpu.SemaphoreType.DMA((3,)),
        ],
        compiler_params=pltpu.CompilerParams(vmem_limit_bytes=(8 if direct else 56) * 2**20),
        cost_estimate=pl.CostEstimate(flops=2**22, bytes_accessed=2**21, transcendentals=0),
        name="prepare",
    )(
        pair_count,
        scalars,
        *(pltpu.with_memory_space_constraint(here, pltpu.HBM) for here in lists),
        *cell_parts,
    )

    def forward(*refs):
        forward_kernel(len(station_parts), direct, *refs)

    out_shape = [
        jax.ShapeDtypeStruct((5 * rows + (6 * own // 128 if direct else 0), 128), F32),
        jax.ShapeDtypeStruct((16, width), F32),
    ]
    if direct:
        out_shape += [
            jax.ShapeDtypeStruct((extent, width), BF16),
            jax.ShapeDtypeStruct((extent, width), F8),
        ]
    image_part, station_all, *kept = pl.pallas_call(
        forward,
        out_shape=out_shape,
        in_specs=[in_vmem] * (1 + len(prepared) + len(station_parts)),
        out_specs=[in_vmem] * len(out_shape),
        scratch_shapes=[
            pltpu.VMEM((DEPTH, width), F32),
            pltpu.VMEM((DEPTH, width), BF16),
            pltpu.VMEM((blocks, 16, width), F32),
            pltpu.VMEM((13 * rows, 128), F32),
        ],
        compiler_params=params,
        name="forward",
    )(count, *prepared, *station_parts)
    if direct:
        image_parts = exchanged(image_part, "cell", cell_size)
    else:
        image_parts = [lax.psum(image_part, "cell")]

    def adjoint(*refs):
        (kept_adjoint_kernel if direct else adjoint_kernel)(*refs)

    if direct:
        scratch = [pltpu.VMEM((8, width), F32)]
    else:
        scratch = [
            pltpu.VMEM((DEPTH, width), F32),
            pltpu.VMEM((DEPTH, extent), F32),
            pltpu.VMEM((width, DEPTH), BF16),
            pltpu.VMEM((DEPTH, extent), BF16),
        ]
    partial, image_own = pl.pallas_call(
        adjoint,
        out_shape=(
            jax.ShapeDtypeStruct((2 * blocks, CELLS + 128), F32),
            jax.ShapeDtypeStruct((8, own if direct else width), F32),
        ),
        in_specs=[in_vmem] * (3 + len(kept) + len(image_parts)),
        out_specs=(in_vmem, in_vmem),
        scratch_shapes=[
            pltpu.VMEM((8, width), F32),
            *scratch,
            pltpu.VMEM((24, width), F32),
        ],
        compiler_params=params,
        name="adjoint",
    )(count, station_all, cell_all, *kept, *image_parts)
    if not direct:
        image_own = lax.dynamic_slice_in_dim(image_own, lax.axis_index("cell") * own, own, axis=1)
    partial_parts = exchanged(partial, "stn", stn_size)

    def update(*refs):
        update_kernel(stn_size, *refs)

    flat = direction.reshape(-1, 128)
    densities_next, residual_next, gradient, norm_part = pl.pallas_call(
        update,
        out_shape=(
            jax.ShapeDtypeStruct(flat.shape, F32),
            jax.ShapeDtypeStruct(residual.shape, F32),
            jax.ShapeDtypeStruct(flat.shape, F32),
            jax.ShapeDtypeStruct((1, 128), F32),
        ),
        in_specs=[in_vmem] * (5 + stn_size),
        out_specs=(in_vmem,) * 4,
        compiler_params=small,
        name="update",
    )(last_norm, densities.reshape(flat.shape), flat, residual, image_own, *partial_parts)
    if direct:
        norm_parts = exchanged(norm_part, "cell", cell_size)
    else:
        norm_parts = [lax.psum(norm_part, "cell")]
    direction_next, norm_next = pl.pallas_call(
        finish_kernel,
        out_shape=(
            jax.ShapeDtypeStruct(flat.shape, F32),
            jax.ShapeDtypeStruct((1,), F32),
        ),
        in_specs=[in_vmem] * (3 + len(norm_parts)),
        out_specs=(in_vmem, in_smem),
        compiler_params=small,
        name="finish",
    )(last_norm, gradient, flat, *norm_parts)
    return (densities_next.reshape(-1), residual_next, direction_next.reshape(-1), norm_next)


def solution(mesh):
    in_specs = (
        P(("survey", "cell", "stn")),
        P(None, ("survey", "cell", "stn")),
        P(("survey", "cell", "stn")),
        P("survey"),
        P(None, ("survey", "cell", "stn")),
        P(None, ("survey", "cell", "stn")),
        P(("survey", "cell"), "stn", None),
        P(("survey", "cell"), "stn", None),
        P(("survey", "cell"), "stn"),
    )
    out_specs = (
        P(("survey", "cell", "stn")),
        P(None, ("survey", "cell", "stn")),
        P(("survey", "cell", "stn")),
        P("survey"),
    )
    return jax.shard_map(
        on_device, mesh=mesh, in_specs=in_specs, out_specs=out_specs, check_vma=False
    )
```
